32 devices in a mesh: grp: 4 (over z), col: 8 (over y, x, core).
Axes of the slice: x: 2, y: 2, z: 4, core: 2. Of those that a mesh axis runs over, the one named last changes fastest.
Arguments:
- descriptors: bfloat16 [10, 32, 32, 1024], P(None, None, 'grp', 'col'), may hold values from -6 to 6
- solid_temp: float32 [32, 32, 1024], P(None, 'grp', 'col'), may hold values from -6 to 6
- fluid_temp: float32 [32, 32, 1024], P(None, 'grp', 'col'), may hold values from -6 to 6
- material: int32 [32, 32, 1024], P(None, 'grp', 'col'), may hold values from 0 to 3
- fixed_mask: int32 [32, 32, 1024], P(None, 'grp', 'col'), may hold values 0 or 1
- solid_cond: float32 [4], replicated, may hold values from 0.3 to 1.5
- fluid_cond: float32 [4], replicated, may hold values from 0.3 to 1.5
- w_in: bfloat16 [12, 64], replicated, may hold values from -1.75 to 1.75
- b_in: float32 [64], replicated, may hold values from -3 to 3
- w_mid: bfloat16 [64, 64], replicated, may hold values from -0.75 to 0.75
- b_mid: float32 [64], replicated, may hold values from -3 to 3
- w_out: bfloat16 [64, 2], replicated, may hold values from -0.75 to 0.75
- b_out: float32 [2], replicated, may hold values from -3 to 3
- solid_cot: float32 [32, 32, 1024], P(None, 'grp', 'col'), may hold values from -18 to 18
- fluid_cot: float32 [32, 32, 1024], P(None, 'grp', 'col'), may hold values from -18 to 18
Outputs:
- adj_solid: float32 [32, 32, 1024], P(None, 'grp', 'col')
- adj_fluid: float32 [32, 32, 1024], P(None, 'grp', 'col')
- grad_w_in: float32 [12, 64], replicated
- grad_b_in: float32 [64], replicated
- grad_w_mid: float32 [64, 64], replicated
- grad_b_mid: float32 [64], replicated
- grad_w_out: float32 [64, 2], replicated
- grad_b_out: float32 [2], replicated
The draws below stay inside these ranges and needn't reach their ends.
All inputs are finite; a program needn't handle non-finite values. No bound on the sum of `fixed_mask` on one device may be relied on, other than what follows from the above.
Results may differ from the reference program's by a relative error of at most 0.01.
The reference program's roundings to bfloat16 on the way (of `features`, `hidden_one`, `hidden_two` and `d_logits`) count: a program that leaves them out, or rounds other values in their place, can miss the bound.
Values sent between devices are 32-bit elements; how exact they have to be, the bound alone decides.
A program may use at most 64 MiB of HBM per device.

```python
import math
import jax
import jax.numpy as jnp
from jax import lax

FEAT = 12
DESC = 10
HID = 64
NMAT = 4
NX = 32
NY = 1024
NZ = 32


def plant(result, own_key, least, largest):
    longest = result.shape.index(max(result.shape))
    spots = []
    for shift in (0, 1):
        where = [jax.random.randint(jax.random.fold_in(own_key, axis), (), 0, length) for axis, length in enumerate(result.shape)]
        where[longest] = (where[longest] + shift) % result.shape[longest]
        spots.append(tuple(where))
    return result.at[spots[0]].set(least).at[spots[1]].set(largest)


def steps_of(key, extent, pieces, least, top_value):
    def one(position, parts):
        draws = jax.random.uniform(jax.random.fold_in(jax.random.fold_in(key, 6), position), (parts,), jnp.float32, least / len(pieces), top_value / len(pieces))
        return jnp.repeat(jnp.exp(draws), extent[position] // parts).reshape((-1,) + (1,) * (len(extent) - position - 1))

    gain = one(*pieces[0])
    for cut in pieces[1:]:
        gain = gain * one(*cut)
    return gain


def scatter_about(key, dims, scale, reach, shards=(), kind=jnp.bfloat16):
    entries = scale * jax.random.normal(key, dims, jnp.float32)
    if shards:
        entries = entries * steps_of(key, dims, shards, -0.22, 0.18)
    return jnp.clip(entries, -reach, reach).astype(kind)


def setup_inputs(seed: int = 0) -> dict:
    splits = jax.random.split(jax.random.key(seed), 16)
    return {
        "descriptors": scatter_about(splits[0], (DESC, NZ, NX, NY), 1.0, 6.0, ((2, 4), (3, 8))),
        "solid_temp": scatter_about(splits[1], (NZ, NX, NY), 1.0, 6.0, ((1, 4), (2, 8)), jnp.float32),
        "fluid_temp": scatter_about(splits[2], (NZ, NX, NY), 1.0, 6.0, ((1, 4), (2, 8)), jnp.float32),
        "material": plant(jax.random.randint(splits[3], (NZ, NX, NY), 0, NMAT), jax.random.fold_in(splits[3], 1), 0, NMAT - 1).astype(jnp.int32),
        "fixed_mask": plant((jax.random.randint(splits[4], (NZ, NX, NY), 0, 8) < 1).astype(jnp.int32), jax.random.fold_in(splits[4], 1), 0, 1),
        "solid_cond": jnp.clip(jnp.exp(jax.random.uniform(splits[5], (NMAT,), jnp.float32, math.log(0.3), math.log(1.5))), 0.3, 1.5),
        "fluid_cond": jnp.clip(jnp.exp(jax.random.uniform(splits[6], (NMAT,), jnp.float32, math.log(0.3), math.log(1.5))), 0.3, 1.5),
        "w_in": scatter_about(splits[7], (FEAT, HID), FEAT ** -0.5, 1.75),
        "b_in": scatter_about(splits[8], (HID,), 0.5, 3.0, (), jnp.float32),
        "w_mid": scatter_about(splits[9], (HID, HID), HID ** -0.5, 0.75),
        "b_mid": scatter_about(splits[10], (HID,), 0.5, 3.0, (), jnp.float32),
        "w_out": scatter_about(splits[11], (HID, 2), HID ** -0.5, 0.75),
        "b_out": scatter_about(splits[12], (2,), 0.5, 3.0, (), jnp.float32),
        "solid_cot": scatter_about(splits[13], (NZ, NX, NY), 3.0, 18.0, ((1, 4), (2, 8)), jnp.float32),
        "fluid_cot": scatter_about(splits[14], (NZ, NX, NY), 3.0, 18.0, ((1, 4), (2, 8)), jnp.float32),
    }


time_step = 0.15
loss_gain = 16.0

def material_lookup(material, lookup_table):
    summed = jnp.zeros(material.shape, jnp.float32)
    for material_kind in range(lookup_table.shape[0]):
        summed = summed + jnp.where(material == material_kind, lookup_table[material_kind], 0.0)
    return summed

def neighbour_sum(padded, values_field):
    return padded[:, :, 2:, 1:-1] + padded[:, :, :-2, 1:-1] + padded[:, :, 1:-1, 2:] + padded[:, :, 1:-1, :-2] - 4.0 * values_field

def laplace(values_field):
    padded = jnp.pad(values_field, ((0, 0), (0, 0), (1, 1), (1, 1)))
    return neighbour_sum(padded, values_field)

def network(features, w_in, b_in, w_mid, b_mid, w_out, b_out):
    hidden_one = jnp.tanh(jnp.dot(w_in.T, features, preferred_element_type=jnp.float32) + b_in[:, None]).astype(jnp.bfloat16)
    hidden_two = jnp.tanh(jnp.dot(w_mid.T, hidden_one, preferred_element_type=jnp.float32) + b_mid[:, None]).astype(jnp.bfloat16)
    logits = jnp.dot(w_out.T, hidden_two, preferred_element_type=jnp.float32) + b_out[:, None]
    return (hidden_one, hidden_two, logits)

def coupling_terms(logits):
    transfer_coef = jax.nn.softplus(logits[0])
    area_coef = jax.nn.softplus(logits[1])
    return (transfer_coef * area_coef, transfer_coef, area_coef)

def backprop(features, hidden_one, hidden_two, logits, d_coupling, w_in, w_mid, w_out):
    coupling, transfer_coef, area_coef = coupling_terms(logits)
    d_logits = jnp.stack([d_coupling * area_coef * jax.nn.sigmoid(logits[0]), d_coupling * transfer_coef * jax.nn.sigmoid(logits[1])]).astype(jnp.bfloat16)
    d_hidden_two = (jnp.dot(w_out, d_logits, preferred_element_type=jnp.float32) * (1.0 - jnp.square(hidden_two.astype(jnp.float32)))).astype(jnp.bfloat16)
    d_hidden_one = (jnp.dot(w_mid, d_hidden_two, preferred_element_type=jnp.float32) * (1.0 - jnp.square(hidden_one.astype(jnp.float32)))).astype(jnp.bfloat16)
    d_features = jnp.dot(w_in[w_in.shape[0] - 2:], d_hidden_one, preferred_element_type=jnp.float32)
    gradients = (jnp.dot(features, d_hidden_one.T, preferred_element_type=jnp.float32), lax.optimization_barrier(jnp.sum(d_hidden_one.astype(jnp.float32), axis=1)), jnp.dot(hidden_one, d_hidden_two.T, preferred_element_type=jnp.float32), lax.optimization_barrier(jnp.sum(d_hidden_two.astype(jnp.float32), axis=1)), jnp.dot(hidden_two, d_logits.T, preferred_element_type=jnp.float32), lax.optimization_barrier(jnp.sum(d_logits.astype(jnp.float32), axis=1)))
    return (coupling, d_features, gradients)

def build_features(desc_line, solid_line, fluid_line):
    cells = solid_line.size
    return jnp.concatenate([desc_line.reshape(desc_line.shape[0], cells), solid_line.reshape(1, cells).astype(jnp.bfloat16), fluid_line.reshape(1, cells).astype(jnp.bfloat16)], axis=0)

def forward_coupling(descriptors, solid, fluid, weights):

    def one_line(line_index):
        desc_line = lax.dynamic_index_in_dim(descriptors, line_index, 1, keepdims=False)
        solid_line = lax.dynamic_index_in_dim(solid, line_index, 0, keepdims=False)
        fluid_line = lax.dynamic_index_in_dim(fluid, line_index, 0, keepdims=False)
        features = build_features(desc_line, solid_line, fluid_line)
        logits = network(features, *weights)[2]
        return coupling_terms(logits)[0].reshape(solid_line.shape)
    return lax.map(one_line, jnp.arange(solid.shape[0], dtype=jnp.int32))

def backward_lines(descriptors, solid, fluid, d_coupling, weights, running):
    w_in, b_in, w_mid, b_mid, w_out, b_out = weights

    def one_line(running, line_index):
        desc_line = lax.dynamic_index_in_dim(descriptors, line_index, 1, keepdims=False)
        solid_line = lax.dynamic_index_in_dim(solid, line_index, 0, keepdims=False)
        fluid_line = lax.dynamic_index_in_dim(fluid, line_index, 0, keepdims=False)
        d_line = lax.dynamic_index_in_dim(d_coupling, line_index, 0, keepdims=False)
        features = build_features(desc_line, solid_line, fluid_line)
        hidden_one, hidden_two, logits = network(features, *weights)
        coupling, d_features, gradients = backprop(features, hidden_one, hidden_two, logits, d_line.reshape(-1), w_in, w_mid, w_out)
        running = tuple((left + right for left, right in zip(running, gradients)))
        line_shape = solid_line.shape
        return (running, (coupling.reshape(line_shape), d_features.reshape((2,) + line_shape)))
    running, (coupling, d_features) = lax.scan(one_line, running, jnp.arange(solid.shape[0], dtype=jnp.int32))
    return (running, coupling, jnp.moveaxis(d_features, 1, 0))

def reference(descriptors, solid_temp, fluid_temp, material, fixed_mask, solid_cond, fluid_cond, w_in, b_in, w_mid, b_mid, w_out, b_out, solid_cot, fluid_cot):
    weights = (w_in, b_in, w_mid, b_mid, w_out, b_out)
    conduct = jnp.stack([material_lookup(material, solid_cond), material_lookup(material, fluid_cond)])
    free_cell = 1.0 - fixed_mask.astype(jnp.float32)
    state = jnp.stack([solid_temp, fluid_temp])
    first_coupling = forward_coupling(descriptors, state[0], state[1], weights)
    coupled = first_coupling * (state[1] - state[0])
    later = state + time_step * free_cell * (conduct * laplace(state) + jnp.stack([coupled, -coupled]))
    running = (jnp.zeros((FEAT, HID), jnp.float32), jnp.zeros((HID,), jnp.float32), jnp.zeros((HID, HID), jnp.float32), jnp.zeros((HID,), jnp.float32), jnp.zeros((HID, 2), jnp.float32), jnp.zeros((2,), jnp.float32))
    cotangent = jnp.stack([solid_cot, fluid_cot])
    for section_state in (later, state):
        upstream = time_step * free_cell * cotangent
        pushed = conduct * upstream
        d_coupling = (section_state[1] - section_state[0]) * (upstream[0] - upstream[1])
        running, coupling, d_features = backward_lines(descriptors, section_state[0], section_state[1], d_coupling, weights, running)
        swing_term = coupling * (upstream[1] - upstream[0])
        cotangent = cotangent + laplace(pushed) + jnp.stack([swing_term, -swing_term]) + d_features
    scale = loss_gain / math.sqrt(NX * NY * NZ)
    return (cotangent[0], cotangent[1], running[0] * scale, running[1] * scale, running[2] * scale, running[3] * scale, running[4] * scale, running[5] * scale)
```

```python
import functools
import math

import jax
import jax.numpy as jnp
from jax import lax
from jax.experimental import pallas as pl
from jax.experimental.pallas import tpu as pltpu
from jax.sharding import PartitionSpec as P

time_step = 0.15
loss_gain = 16.0
MESH = pl.DeviceIdType.MESH
f32 = jnp.float32
bf16 = jnp.bfloat16
TILE = 16
LOG = 8


def gates(logit):
    small = jnp.exp(-jnp.abs(logit))
    soft = jnp.maximum(logit, 0.0) + jnp.log1p(small)
    sig = jnp.where(logit >= 0.0, 1.0, small) / (1.0 + small)
    return soft, sig


def kernel(
    ngrp, ncol, scale, zb,
    desc_ref, s_ref, f_ref, mat_ref, mask_ref, scond_ref, fcond_ref,
    w_in_ref, b_in_ref, w_mid_ref, b_mid_ref, w_out_t_ref, b_out_ref, gs_ref, gf_ref,
    adj_s_ref, adj_f_ref, g_w_in_ref, g_b_in_ref, g_w_mid_ref, g_b_mid_ref, g_w_out_ref, g_b_out_ref,
    aug_ref, fd_ref, h1_ref, h2_ref, lg0_ref, lg_ref, free_ref, us_ref, ps_ref, g2_ref,
    halo_ref, grad_ref, xs_ref, xr_ref, ys_ref, yr_ref, xs2_ref, xr2_ref, ys2_ref, yr2_ref,
    acc_ref, part_ref, grp_ref, fin_ref,
    hs_sem, hr_sem, hs2_sem, hr2_sem, c_ssem, c_rsem, g_ssem, g_rsem, a_ssem, a_rsem,
):
    ndesc, nz, nx, ny = desc_ref.shape
    hid = w_mid_ref.shape[0]
    rows = nz * nx
    cells = nx * ny
    row_s, row_one, row_d, row_two = ndesc, ndesc + 2, ndesc + 3, ndesc + 5
    me_g = lax.axis_index("grp")
    me_c = lax.axis_index("col")

    def grp_peer(k):
        return (lax.rem(me_g + (k + ngrp), ngrp), me_c)

    def col_peer(k):
        return (me_g, lax.rem(me_c + (k + ncol), ncol))

    barrier = pltpu.get_barrier_semaphore()
    for k in range(1, ngrp):
        pl.semaphore_signal(barrier, inc=1, device_id=grp_peer(k), device_id_type=MESH)
    for k in range(1, ncol):
        pl.semaphore_signal(barrier, inc=1, device_id=col_peer(k), device_id_type=MESH)

    def remote(src, dst, ssem, rsem, peer):
        return pltpu.make_async_remote_copy(
            src_ref=src, dst_ref=dst, send_sem=ssem, recv_sem=rsem, device_id=peer, device_id_type=MESH
        )

    xi = lax.broadcasted_iota(jnp.int32, (nx, ny), 0)
    yi = lax.broadcasted_iota(jnp.int32, (nx, ny), 1)

    mat = mat_ref[...]
    free = time_step * (1.0 - mask_ref[...].astype(f32))
    free_ref[...] = free
    sk = jnp.zeros((rows, ny), f32)
    fk = jnp.zeros((rows, ny), f32)
    for kind in range(scond_ref.shape[0]):
        sk = sk + jnp.where(mat == kind, scond_ref[kind], 0.0)
        fk = fk + jnp.where(mat == kind, fcond_ref[kind], 0.0)
    us_ref[0:rows, :] = sk * free
    us_ref[rows : 2 * rows, :] = fk * free
    ps_ref[0:rows, :] = us_ref[0:rows, :] * gs_ref[...]
    ps_ref[rows : 2 * rows, :] = us_ref[rows : 2 * rows, :] * gf_ref[...]

    def stage_edges(refs, xsend, ysend):
        for i, (ref, base) in enumerate(refs):
            xsend[0, i] = ref[pl.ds(base, nz, stride=nx), :]
            xsend[1, i] = ref[pl.ds(base + nx - 1, nz, stride=nx), :]
            turned = jnp.transpose(ref[base : base + rows, :])
            ysend[0, i : i + 1, :] = turned[0:1, :]
            ysend[1, i : i + 1, :] = turned[ny - 1 : ny, :]

    def halo_copies(xsend, xrecv, ysend, yrecv, ssem, rsem):
        return [
            remote(xsend.at[0], xrecv.at[0], ssem.at[0], rsem.at[0], grp_peer(-1)),
            remote(xsend.at[1], xrecv.at[1], ssem.at[1], rsem.at[1], grp_peer(1)),
            remote(ysend.at[0], yrecv.at[0], ssem.at[2], rsem.at[2], col_peer(-1)),
            remote(ysend.at[1], yrecv.at[1], ssem.at[3], rsem.at[3], col_peer(1)),
        ]

    not_first_g = jnp.where(me_g == 0, 0.0, 1.0).astype(f32)
    not_last_g = jnp.where(me_g == ngrp - 1, 0.0, 1.0).astype(f32)
    not_first_c = jnp.where(me_c == 0, 0.0, 1.0).astype(f32)
    not_last_c = jnp.where(me_c == ncol - 1, 0.0, 1.0).astype(f32)

    def place_halo(count, xrecv, yrecv):
        line = lax.broadcasted_iota(jnp.int32, (ny, rows), 0)
        for i in range(count):
            low = yrecv[1, i : i + 1, :] * not_first_c
            high = yrecv[0, i : i + 1, :] * not_last_c
            edge = jnp.where(line == 0, low, 0.0) + jnp.where(line == ny - 1, high, 0.0)
            base = i * rows
            halo_ref[base : base + rows, :] = jnp.transpose(edge)
            at_low = pl.ds(base, nz, stride=nx)
            at_high = pl.ds(base + nx - 1, nz, stride=nx)
            halo_ref[at_low, :] = halo_ref[at_low, :] + xrecv[1, i] * not_first_g
            halo_ref[at_high, :] = halo_ref[at_high, :] + xrecv[0, i] * not_last_g

    def lap(v, halo):
        up = jnp.where(xi > 0, pltpu.roll(v, 1, 0), 0.0)
        down = jnp.where(xi < nx - 1, pltpu.roll(v, nx - 1, 0), 0.0)
        left = jnp.where(yi > 0, pltpu.roll(v, 1, 1), 0.0)
        right = jnp.where(yi < ny - 1, pltpu.roll(v, ny - 1, 1), 0.0)
        return (up + down) + (left + right) + halo - 4.0 * v

    stage_edges([(s_ref, 0), (f_ref, 0), (ps_ref, 0), (ps_ref, rows)], xs_ref, ys_ref)
    pl.semaphore_wait(barrier, ngrp + ncol - 2)
    first = halo_copies(xs_ref, xr_ref, ys_ref, yr_ref, hs_sem, hr_sem)
    for copy in first:
        copy.start()

    wide = aug_ref.shape[1]

    def split(b):
        high = b.astype(bf16).astype(f32)
        return high, b - high

    def turned_weights(pieces):
        aug_ref[...] = jnp.zeros(aug_ref.shape, f32)
        for at, value in pieces:
            aug_ref[at : at + value.shape[0], 0:hid] = value
        return jnp.transpose(aug_ref[...])

    b1_high, b1_low = split(b_in_ref[...])
    b2_high, b2_low = split(b_mid_ref[...])
    w_in = w_in_ref[...].astype(f32)
    w_out_t = w_out_t_ref[...].astype(f32)
    turned = turned_weights([(0, w_in), (row_one, b1_high), (row_two, b1_low), (TILE + row_d, w_out_t)])
    w1 = turned[0:hid, 0:TILE].astype(bf16)
    wo = turned[0:hid, TILE : 2 * TILE].astype(bf16)
    turned = turned_weights([(0, w_mid_ref[...].astype(f32)), (hid + row_one, b2_high), (hid + row_two, b2_low)])
    w2 = turned[0:hid, 0 : hid + TILE].astype(bf16)
    wm = w_mid_ref[...]
    aug_ref[...] = jnp.zeros(aug_ref.shape, f32)
    aug_ref[0:2, 0:hid] = w_out_t
    aug_ref[LOG : LOG + 2, 0:hid] = w_in[ndesc : ndesc + 2, :]
    w3 = aug_ref[0:LOG, 0:hid].astype(bf16)
    wd = aug_ref[LOG : 2 * LOG, 0:hid].astype(bf16)
    b_out_0 = b_out_ref[0, 0]
    b_out_1 = b_out_ref[0, 1]

    grad_ref[...] = jnp.zeros(grad_ref.shape, f32)

    def dot(a, b):
        return jnp.dot(a, b, preferred_element_type=f32)

    def set_row(z, row, value):
        fd_ref[pl.ds(pl.multiple_of(z * (nx * TILE), nx * TILE) + row, nx, stride=TILE), :] = value

    def tile(z):
        base = pl.multiple_of(z * (nx * TILE), nx * TILE)
        block = fd_ref[pl.ds(base, nx * TILE), :].astype(bf16)
        return jnp.concatenate([block[x * TILE : (x + 1) * TILE, :] for x in range(nx)], axis=1)

    def put_log(ref, z, value):
        for x in range(nx):
            at = pl.multiple_of(z * (nx * LOG), nx * LOG) + x * LOG
            ref[pl.ds(at, LOG), :] = value[:, x * ny : (x + 1) * ny]

    def get_log(ref, z, row):
        return ref[pl.ds(pl.multiple_of(z * (nx * LOG), nx * LOG) + row, nx, stride=LOG), :]

    def field(ref, z, which=0):
        return ref[pl.ds(pl.multiple_of(z * nx, nx) + which * rows, nx), :]

    def put_field(ref, z, value, which=0):
        ref[pl.ds(pl.multiple_of(z * nx, nx) + which * rows, nx), :] = value

    def layers(fds):
        h1 = [jnp.tanh(dot(w1, fd)).astype(bf16) for fd in fds]
        h2 = [jnp.tanh(dot(w2, jnp.concatenate([h, fd], axis=0))).astype(bf16) for h, fd in zip(h1, fds)]
        logits = [dot(w3, h) for h in h2]
        return h1, h2, logits

    def through(d, h):
        wide_h = h.astype(f32)
        return (d * (1.0 - wide_h * wide_h)).astype(bf16)

    def layers_back(fds, h1, h2, zs):
        d2 = [through(dot(wo, fd), h) for fd, h in zip(fds, h2)]
        d1 = [through(dot(wm, d), h) for d, h in zip(d2, h1)]
        for z, d in zip(zs, d1):
            put_log(lg_ref, z, dot(wd, d))
        total = grad_ref[:, 0 : 3 * hid + TILE]
        for i in range(len(zs)):
            left = jnp.concatenate([fds[i], h1[i]], axis=0)
            right = jnp.concatenate([d1[i], d2[i], h2[i], fds[i]], axis=0)
            total = total + lax.dot_general(
                left, right, (((1,), (1,)), ((), ())), preferred_element_type=f32
            )
        grad_ref[:, 0 : 3 * hid + TILE] = total

    ones = jnp.ones((nx, ny), f32)
    nil = jnp.zeros((nx, ny), f32)

    def start_body(step, _):
        zs = [step * zb + i for i in range(zb)]
        for z in zs:
            for d in range(ndesc):
                set_row(z, d, desc_ref[d, z].astype(f32))
            set_row(z, row_s, field(s_ref, z))
            set_row(z, row_s + 1, field(f_ref, z))
            set_row(z, row_one, ones)
            set_row(z, row_d, nil)
            set_row(z, row_d + 1, nil)
            set_row(z, row_two, ones)
        fds = [tile(z) for z in zs]
        h1, h2, logits = layers(fds)
        for z, a, b, c in zip(zs, h1, h2, logits):
            h1_ref[z] = a
            h2_ref[z] = b
            put_log(lg0_ref, z, c)
        return 0

    lax.fori_loop(0, nz // zb, start_body, 0)

    for copy in first:
        copy.wait()
    place_halo(4, xr_ref, yr_ref)

    def logit_cots(z, dcoup, ref):
        h_sf, h_sig = gates(get_log(ref, z, 0) + b_out_0)
        a_sf, a_sig = gates(get_log(ref, z, 1) + b_out_1)
        set_row(z, row_d, dcoup * a_sf * h_sig)
        set_row(z, row_d + 1, dcoup * h_sf * a_sig)
        return h_sf * a_sf

    def later_body(step, _):
        zs = [step * zb + i for i in range(zb)]
        diff = []
        for z in zs:
            h_sf = gates(get_log(lg0_ref, z, 0) + b_out_0)[0]
            a_sf = gates(get_log(lg0_ref, z, 1) + b_out_1)[0]
            solid, fluid, free = field(s_ref, z), field(f_ref, z), field(free_ref, z)
            swap = free * (h_sf * a_sf) * (fluid - solid)
            solid_1 = solid + field(us_ref, z) * lap(solid, field(halo_ref, z)) + swap
            fluid_1 = fluid + field(us_ref, z, 1) * lap(fluid, field(halo_ref, z, 1)) - swap
            set_row(z, row_s, solid_1)
            set_row(z, row_s + 1, fluid_1)
            diff.append(fluid_1 - solid_1)
        fds = [tile(z) for z in zs]
        h1, h2, logits = layers(fds)
        for z, c in zip(zs, logits):
            put_log(lg_ref, z, c)
        swing = []
        for z, d in zip(zs, diff):
            turn = field(free_ref, z) * (field(gs_ref, z) - field(gf_ref, z))
            swing.append(logit_cots(z, d * turn, lg_ref) * turn)
        fds = [tile(z) for z in zs]
        layers_back(fds, h1, h2, zs)
        for z, w in zip(zs, swing):
            new_s = field(gs_ref, z) + lap(field(ps_ref, z), field(halo_ref, z, 2)) - w + get_log(lg_ref, z, 0)
            new_f = field(gf_ref, z) + lap(field(ps_ref, z, 1), field(halo_ref, z, 3)) + w + get_log(lg_ref, z, 1)
            put_field(g2_ref, z, new_s)
            put_field(g2_ref, z, new_f, 1)
            put_field(ps_ref, z, field(us_ref, z) * new_s)
            put_field(ps_ref, z, field(us_ref, z, 1) * new_f, 1)
        return 0

    lax.fori_loop(0, nz // zb, later_body, 0)

    stage_edges([(ps_ref, 0), (ps_ref, rows)], xs2_ref, ys2_ref)
    second = halo_copies(xs2_ref, xr2_ref, ys2_ref, yr2_ref, hs2_sem, hr2_sem)
    for copy in second:
        copy.start()

    def first_body(step, _):
        zs = [step * zb + i for i in range(zb)]
        swing = []
        for z in zs:
            solid, fluid = field(s_ref, z), field(f_ref, z)
            set_row(z, row_s, solid)
            set_row(z, row_s + 1, fluid)
            turn = field(free_ref, z) * (field(g2_ref, z) - field(g2_ref, z, 1))
            swing.append(logit_cots(z, (fluid - solid) * turn, lg0_ref) * turn)
        fds = [tile(z) for z in zs]
        layers_back(fds, [h1_ref[z] for z in zs], [h2_ref[z] for z in zs], zs)
        for z, w in zip(zs, swing):
            put_field(g2_ref, z, field(g2_ref, z) - w + get_log(lg_ref, z, 0))
            put_field(g2_ref, z, field(g2_ref, z, 1) + w + get_log(lg_ref, z, 1), 1)
        return 0

    lax.fori_loop(0, nz // zb, first_body, 0)

    piece = acc_ref.shape[1]
    lane = lax.broadcasted_iota(jnp.int32, (hid // 2, 2 * hid), 1)
    half = hid // 2
    wide_l = 2 * hid
    packed = jnp.concatenate(
        [
            grad_ref[0:TILE, 0:wide_l],
            jnp.where(
                lane >= hid,
                grad_ref[TILE : TILE + half, 0:wide_l],
                pltpu.roll(grad_ref[TILE + half : TILE + hid, 0:wide_l], hid, 1),
            ),
            grad_ref[TILE - LOG : TILE, wide_l : 2 * wide_l],
            jnp.zeros((ncol * piece - TILE - half - LOG, wide_l), f32),
        ],
        axis=0,
    )
    for i in range(ncol):
        acc_ref[i] = packed[i * piece : (i + 1) * piece, :]
    sends = []
    for k in range(1, ncol):
        dev = col_peer(k)
        sends.append(remote(acc_ref.at[dev[1]], part_ref.at[k - 1], c_ssem.at[k - 1], c_rsem.at[k - 1], dev))
    for copy in sends:
        copy.start()

    for copy in second:
        copy.wait()
    place_halo(2, xr2_ref, yr2_ref)

    for copy in sends:
        copy.wait()
    own = acc_ref[me_c]
    for k in range(ncol - 1):
        own = own + part_ref[k]
    grp_ref[me_g] = own
    sends = []
    for k in range(1, ngrp):
        sends.append(
            remote(grp_ref.at[me_g], grp_ref.at[me_g], g_ssem.at[k - 1], g_rsem.at[k - 1], grp_peer(k))
        )
    for copy in sends:
        copy.start()

    def final_body(z, _):
        adj_s_ref[pl.ds(pl.multiple_of(z * nx, nx), nx), :] = field(g2_ref, z) + lap(
            field(ps_ref, z), field(halo_ref, z)
        )
        adj_f_ref[pl.ds(pl.multiple_of(z * nx, nx), nx), :] = field(g2_ref, z, 1) + lap(
            field(ps_ref, z, 1), field(halo_ref, z, 1)
        )
        return 0

    lax.fori_loop(0, nz, final_body, 0, unroll=zb)

    for copy in sends:
        copy.wait()
    own = grp_ref[0]
    for k in range(1, ngrp):
        own = own + grp_ref[k]
    fin_ref[me_c] = own * scale
    sends = []
    for k in range(1, ncol):
        sends.append(remote(fin_ref.at[me_c], fin_ref.at[me_c], a_ssem.at[k - 1], a_rsem.at[k - 1], col_peer(k)))
    for copy in sends:
        copy.start()
    for copy in sends:
        copy.wait()
    whole = jnp.concatenate([fin_ref[i] for i in range(ncol)], axis=0)
    g_w_in_ref[...] = whole[0 : ndesc + 2, 0:hid]
    ones_row = whole[row_one : row_one + 1, :]
    g_b_in_ref[...] = ones_row[:, 0:hid]
    g_b_mid_ref[...] = pltpu.roll(ones_row, hid, 1)[:, 0:hid]
    mid = whole[TILE : TILE + half, :]
    g_w_mid_ref[0:half, :] = pltpu.roll(mid, hid, 1)[:, 0:hid]
    g_w_mid_ref[half:hid, :] = mid[:, 0:hid]
    at = TILE + half + row_d - (TILE - LOG)
    g_w_out_ref[...] = whole[at : at + 2, 0:hid]
    one_lane = hid + row_one
    b0 = pltpu.roll(whole[at : at + 1, :], wide_l - one_lane, 1)
    b1 = pltpu.roll(whole[at + 1 : at + 2, :], wide_l - one_lane + 1, 1)
    first_lane = lax.broadcasted_iota(jnp.int32, (1, wide_l), 1) == 0
    g_b_out_ref[...] = jnp.where(first_lane, b0, b1)[:, 0:2]


def solution(mesh):
    ngrp, ncol = mesh.shape["grp"], mesh.shape["col"]

    def shards(
        descriptors, solid_temp, fluid_temp, material, fixed_mask, solid_cond, fluid_cond,
        w_in, b_in, w_mid, b_mid, w_out, b_out, solid_cot, fluid_cot,
    ):
        ndesc, nz, nx, ny = descriptors.shape
        feat, hid = w_in.shape
        rows = nz * nx
        zb = next(k for k in (4, 2, 1) if nz % k == 0)
        scale = loss_gain / math.sqrt(rows * ny * ngrp * ncol)
        used = TILE + hid // 2 + LOG
        piece = 8 * -(-used // (8 * ncol))
        flat = lambda a: a.reshape(rows, ny)
        vmem = pl.BlockSpec(memory_space=pltpu.VMEM)
        smem = pl.BlockSpec(memory_space=pltpu.SMEM)
        sds = jax.ShapeDtypeStruct
        outs = pl.pallas_call(
            functools.partial(kernel, ngrp, ncol, scale, zb),
            out_shape=(
                sds((rows, ny), f32), sds((rows, ny), f32), sds((feat, hid), f32), sds((1, hid), f32),
                sds((hid, hid), f32), sds((1, hid), f32), sds((2, hid), f32), sds((1, 2), f32),
            ),
            in_specs=[vmem] * 5 + [smem] * 2 + [vmem] * 5 + [smem] + [vmem] * 2,
            out_specs=(vmem,) * 8,
            scratch_shapes=[
                pltpu.VMEM((128, 128), f32),
                pltpu.VMEM((rows * TILE, ny), f32),
                pltpu.VMEM((nz, hid, nx * ny), bf16),
                pltpu.VMEM((nz, hid, nx * ny), bf16),
                pltpu.VMEM((rows * LOG, ny), f32),
                pltpu.VMEM((rows * LOG, ny), f32),
                pltpu.VMEM((rows, ny), f32),
                pltpu.VMEM((2 * rows, ny), f32),
                pltpu.VMEM((2 * rows, ny), f32),
                pltpu.VMEM((2 * rows, ny), f32),
                pltpu.VMEM((4 * rows, ny), f32),
                pltpu.VMEM((TILE + hid, 4 * hid), f32),
                pltpu.VMEM((2, 4, nz, ny), f32),
                pltpu.VMEM((2, 4, nz, ny), f32),
                pltpu.VMEM((2, 4, rows), f32),
                pltpu.VMEM((2, 4, rows), f32),
                pltpu.VMEM((2, 2, nz, ny), f32),
                pltpu.VMEM((2, 2, nz, ny), f32),
                pltpu.VMEM((2, 2, rows), f32),
                pltpu.VMEM((2, 2, rows), f32),
                pltpu.VMEM((ncol, piece, 2 * hid), f32),
                pltpu.VMEM((ncol - 1, piece, 2 * hid), f32),
                pltpu.VMEM((ngrp, piece, 2 * hid), f32),
                pltpu.VMEM((ncol, piece, 2 * hid), f32),
                pltpu.SemaphoreType.DMA((4,)),
                pltpu.SemaphoreType.DMA((4,)),
                pltpu.SemaphoreType.DMA((4,)),
                pltpu.SemaphoreType.DMA((4,)),
                pltpu.SemaphoreType.DMA((ncol - 1,)),
                pltpu.SemaphoreType.DMA((ncol - 1,)),
                pltpu.SemaphoreType.DMA((ngrp - 1,)),
                pltpu.SemaphoreType.DMA((ngrp - 1,)),
                pltpu.SemaphoreType.DMA((ncol - 1,)),
                pltpu.SemaphoreType.DMA((ncol - 1,)),
            ],
            compiler_params=pltpu.CompilerParams(
                collective_id=0, has_side_effects=True, vmem_limit_bytes=48 * 1024 * 1024
            ),
            name="wick_adjoint",
        )(
            descriptors, flat(solid_temp), flat(fluid_temp), flat(material), flat(fixed_mask),
            solid_cond, fluid_cond, w_in, b_in.reshape(1, hid), w_mid, b_mid.reshape(1, hid),
            w_out.T, b_out.reshape(1, 2), flat(solid_cot), flat(fluid_cot),
        )
        block = lambda a: a.reshape(nz, nx, ny)
        return (
            block(outs[0]), block(outs[1]), outs[2], outs[3].reshape(hid),
            outs[4], outs[5].reshape(hid), outs[6].T, outs[7].reshape(2),
        )

    plane = P(None, "grp", "col")
    return jax.shard_map(
        shards,
        mesh=mesh,
        in_specs=(P(None, None, "grp", "col"),) + (plane,) * 4 + (P(),) * 8 + (plane,) * 2,
        out_specs=(plane, plane) + (P(),) * 6,
        check_vma=False,
    )
```

```python
import functools
import math

import jax
import jax.numpy as jnp
from jax import lax
from jax.experimental import pallas as pl
from jax.experimental.pallas import tpu as pltpu
from jax.sharding import PartitionSpec as P

time_step = 0.15
loss_gain = 16.0
MESH = pl.DeviceIdType.MESH
f32 = jnp.float32
bf16 = jnp.bfloat16
TILE = 16
LOG = 8
FETCHED = 13


def gates(logit):
    small = jnp.exp(-jnp.abs(logit))
    soft = jnp.maximum(logit, 0.0) + jnp.log1p(small)
    sig = jnp.where(logit >= 0.0, 1.0, small) / (1.0 + small)
    return soft, sig


def kernel(
    ngrp, ncol, scale, zb,
    w_in_ref, w_out_t_ref, *refs,
):
    sources, rest = refs[:FETCHED], refs[FETCHED:]
    (
    out_s_ref, out_f_ref, whole_ref, adj_s_ref, adj_f_ref, out_sem,
    mask_ref, mat_ref, scond_ref, fcond_ref, gs_ref, gf_ref, s_ref, f_ref,
    b_in_ref, b_mid_ref, w_mid_ref, b_out_ref, desc_ref, in_sem,
    aug_ref, fd_ref, h1_ref, h2_ref, lg0_ref, lg_ref, free_ref, us_ref, ps_ref, g2_ref,
    halo_ref, grad_ref, xs_ref, xr_ref, ys_ref, yr_ref, xs2_ref, xr2_ref, ys2_ref, yr2_ref,
    acc_ref, part_ref, grp_ref, fin_ref,
    hs_sem, hr_sem, hs2_sem, hr2_sem, c_ssem, c_rsem, g_ssem, g_rsem, a_ssem, a_rsem,
    ) = rest
    held = (
        mask_ref, mat_ref, scond_ref, fcond_ref, gs_ref, gf_ref, s_ref, f_ref,
        b_in_ref, b_mid_ref, w_mid_ref, b_out_ref, desc_ref,
    )
    fetches = [
        pltpu.make_async_copy(source, place, in_sem.at[i])
        for i, (source, place) in enumerate(zip(sources, held))
    ]
    for fetch in fetches:
        fetch.start()
    ndesc, _, ny = desc_ref.shape
    nz = xs_ref.shape[2]
    nx = s_ref.shape[0] // nz
    hid = w_mid_ref.shape[0]
    rows = nz * nx
    xw = max(1, 2 * 128 // ny)
    xw = xw if nx % xw == 0 else 1
    row_s, row_one, row_d, row_two = ndesc, ndesc + 2, ndesc + 3, ndesc + 5
    me_g = lax.axis_index("grp")
    me_c = lax.axis_index("col")

    def grp_peer(k):
        return (lax.rem(me_g + (k + ngrp), ngrp), me_c)

    def col_peer(k):
        return (me_g, lax.rem(me_c + (k + ncol), ncol))

    barrier = pltpu.get_barrier_semaphore()
    for k in range(1, ngrp):
        pl.semaphore_signal(barrier, inc=1, device_id=grp_peer(k), device_id_type=MESH)
    for k in range(1, ncol):
        pl.semaphore_signal(barrier, inc=1, device_id=col_peer(k), device_id_type=MESH)

    def remote(src, dst, ssem, rsem, peer):
        return pltpu.make_async_remote_copy(
            src_ref=src, dst_ref=dst, send_sem=ssem, recv_sem=rsem, device_id=peer, device_id_type=MESH
        )

    xi = lax.broadcasted_iota(jnp.int32, (nx, ny), 0)
    yi = lax.broadcasted_iota(jnp.int32, (nx, ny), 1)

    for fetch in fetches[:8]:
        fetch.wait()
    mat = mat_ref[...]
    free = time_step * (1.0 - mask_ref[...].astype(f32))
    free_ref[...] = free
    sk = jnp.zeros((rows, ny), f32)
    fk = jnp.zeros((rows, ny), f32)
    for kind in range(scond_ref.shape[1]):
        sk = sk + jnp.where(mat == kind, scond_ref[0:1, kind : kind + 1], 0.0)
        fk = fk + jnp.where(mat == kind, fcond_ref[0:1, kind : kind + 1], 0.0)
    us_ref[0:rows, :] = sk * free
    us_ref[rows : 2 * rows, :] = fk * free
    ps_ref[0:rows, :] = us_ref[0:rows, :] * gs_ref[...]
    ps_ref[rows : 2 * rows, :] = us_ref[rows : 2 * rows, :] * gf_ref[...]

    def stage_edges(refs, xsend, ysend):
        for i, (ref, base) in enumerate(refs):
            xsend[0, i] = ref[pl.ds(base, nz, stride=nx), :]
            xsend[1, i] = ref[pl.ds(base + nx - 1, nz, stride=nx), :]
            turned = jnp.transpose(ref[base : base + rows, :])
            ysend[0, i : i + 1, :] = turned[0:1, :]
            ysend[1, i : i + 1, :] = turned[ny - 1 : ny, :]

    def halo_copies(xsend, xrecv, ysend, yrecv, ssem, rsem):
        return [
            remote(xsend.at[0], xrecv.at[0], ssem.at[0], rsem.at[0], grp_peer(-1)),
            remote(xsend.at[1], xrecv.at[1], ssem.at[1], rsem.at[1], grp_peer(1)),
            remote(ysend.at[0], yrecv.at[0], ssem.at[2], rsem.at[2], col_peer(-1)),
            remote(ysend.at[1], yrecv.at[1], ssem.at[3], rsem.at[3], col_peer(1)),
        ]

    not_first_g = jnp.where(me_g == 0, 0.0, 1.0).astype(f32)
    not_last_g = jnp.where(me_g == ngrp - 1, 0.0, 1.0).astype(f32)
    not_first_c = jnp.where(me_c == 0, 0.0, 1.0).astype(f32)
    not_last_c = jnp.where(me_c == ncol - 1, 0.0, 1.0).astype(f32)

    def place_halo(count, xrecv, yrecv):
        line = lax.broadcasted_iota(jnp.int32, (ny, rows), 0)
        for i in range(count):
            low = yrecv[1, i : i + 1, :] * not_first_c
            high = yrecv[0, i : i + 1, :] * not_last_c
            edge = jnp.where(line == 0, low, 0.0) + jnp.where(line == ny - 1, high, 0.0)
            base = i * rows
            halo_ref[base : base + rows, :] = jnp.transpose(edge)
            at_low = pl.ds(base, nz, stride=nx)
            at_high = pl.ds(base + nx - 1, nz, stride=nx)
            halo_ref[at_low, :] = halo_ref[at_low, :] + xrecv[1, i] * not_first_g
            halo_ref[at_high, :] = halo_ref[at_high, :] + xrecv[0, i] * not_last_g

    def lap(v, halo):
        up = jnp.where(xi > 0, pltpu.roll(v, 1, 0), 0.0)
        down = jnp.where(xi < nx - 1, pltpu.roll(v, nx - 1, 0), 0.0)
        left = jnp.where(yi > 0, pltpu.roll(v, 1, 1), 0.0)
        right = jnp.where(yi < ny - 1, pltpu.roll(v, ny - 1, 1), 0.0)
        return (up + down) + (left + right) + halo - 4.0 * v

    stage_edges([(s_ref, 0), (f_ref, 0), (ps_ref, 0), (ps_ref, rows)], xs_ref, ys_ref)
    pl.semaphore_wait(barrier, ngrp + ncol - 2)
    first = halo_copies(xs_ref, xr_ref, ys_ref, yr_ref, hs_sem, hr_sem)
    for copy in first:
        copy.start()

    for fetch in fetches[8:]:
        fetch.wait()
    wide = aug_ref.shape[1]

    def split(b):
        high = b.astype(bf16).astype(f32)
        return high, b - high

    def turned_weights(pieces):
        aug_ref[...] = jnp.zeros(aug_ref.shape, f32)
        for at, value in pieces:
            aug_ref[at : at + value.shape[0], 0:hid] = value
        return jnp.transpose(aug_ref[...])

    b1_high, b1_low = split(b_in_ref[...])
    b2_high, b2_low = split(b_mid_ref[...])
    w_in = w_in_ref[...].astype(f32)
    w_out_t = w_out_t_ref[...].astype(f32)
    turned = turned_weights([(0, w_in), (row_one, b1_high), (row_two, b1_low), (TILE + row_d, w_out_t)])
    w1 = turned[0:hid, 0:TILE].astype(bf16)
    wo = turned[0:hid, TILE : 2 * TILE].astype(bf16)
    turned = turned_weights([(0, w_mid_ref[...].astype(f32)), (hid + row_one, b2_high), (hid + row_two, b2_low)])
    w2 = turned[0:hid, 0 : hid + TILE].astype(bf16)
    wm = w_mid_ref[...]
    aug_ref[...] = jnp.zeros(aug_ref.shape, f32)
    aug_ref[0:2, 0:hid] = w_out_t
    aug_ref[LOG : LOG + 2, 0:hid] = w_in[ndesc : ndesc + 2, :]
    w3 = aug_ref[0:LOG, 0:hid].astype(bf16)
    wd = aug_ref[LOG : 2 * LOG, 0:hid].astype(bf16)
    b_out_0 = jnp.broadcast_to(b_out_ref[0:1, 0:1], (nx, ny))
    b_out_1 = jnp.broadcast_to(b_out_ref[0:1, 1:2], (nx, ny))

    grad_ref[...] = jnp.zeros(grad_ref.shape, f32)

    def dot(a, b):
        return jnp.dot(a, b, preferred_element_type=f32)

    def set_row(z, row, value):
        fd_ref[pl.ds(pl.multiple_of(z * (nx * TILE), nx * TILE) + row, nx, stride=TILE), :] = value

    def tiles(z):
        base = pl.multiple_of(z * (nx * TILE), nx * TILE)
        block = fd_ref[pl.ds(base, nx * TILE), :].astype(bf16)
        rows_of = [block[x * TILE : (x + 1) * TILE, :] for x in range(nx)]
        return [jnp.concatenate(rows_of[x : x + xw], axis=1) for x in range(0, nx, xw)]

    def put_log(ref, z, chunk, value):
        for x in range(xw):
            at = pl.multiple_of(z * (nx * LOG), nx * LOG) + (chunk * xw + x) * LOG
            ref[pl.ds(at, LOG), :] = value[:, x * ny : (x + 1) * ny]

    def get_log(ref, z, row):
        return ref[pl.ds(pl.multiple_of(z * (nx * LOG), nx * LOG) + row, nx, stride=LOG), :]

    def field(ref, z, which=0):
        return ref[pl.ds(pl.multiple_of(z * nx, nx) + which * rows, nx), :]

    def put_field(ref, z, value, which=0):
        ref[pl.ds(pl.multiple_of(z * nx, nx) + which * rows, nx), :] = value

    def interleave(works, lag):
        left = list(works)
        step = 0
        while any(w is not None for w in left):
            for i, w in enumerate(left):
                if w is not None and step >= i * lag:
                    if next(w, "end") == "end":
                        left[i] = None
            step += 1

    def layers(z, fds, ref, h1, h2):
        n = len(fds)
        for t in range(n + 2):
            if t < n:
                h1.append(jnp.tanh(dot(w1, fds[t])).astype(bf16))
            if 0 <= t - 1 < n:
                both = jnp.concatenate([h1[t - 1], fds[t - 1]], axis=0)
                h2.append(jnp.tanh(dot(w2, both)).astype(bf16))
            if 0 <= t - 2:
                put_log(ref, z, t - 2, dot(w3, h2[t - 2]))
            yield

    def through(d, h):
        wide_h = h.astype(f32)
        return (d * (1.0 - wide_h * wide_h)).astype(bf16)

    def layers_back(z, fds, h1, h2, lefts, rights):
        n = len(fds)
        d1, d2 = [], []
        for t in range(n + 2):
            if t < n:
                d2.append(through(dot(wo, fds[t]), h2[t]))
            if 0 <= t - 1 < n:
                d1.append(through(dot(wm, d2[t - 1]), h1[t - 1]))
            if 0 <= t - 2:
                put_log(lg_ref, z, t - 2, dot(wd, d1[t - 2]))
            yield
        lefts += [jnp.concatenate([a, b], axis=0) for a, b in zip(fds, h1)]
        rights += [jnp.concatenate(parts, axis=0) for parts in zip(d1, d2, h2, fds)]

    def add_terms(lefts, rights):
        grad_ref[:, 0 : 3 * hid + TILE] = grad_ref[:, 0 : 3 * hid + TILE] + lax.dot_general(
            jnp.concatenate(lefts, axis=1),
            jnp.concatenate(rights, axis=1),
            (((1,), (1,)), ((), ())),
            preferred_element_type=f32,
        )

    ones = jnp.ones((nx, ny), f32)
    nil = jnp.zeros((nx, ny), f32)

    def start_body(step, _):
        zs = [step * zb + i for i in range(zb)]
        for d in range(ndesc):
            span = pl.ds(pl.multiple_of(step * (zb * nx), zb * nx), zb * nx)
            lines = desc_ref[d, span, :].astype(f32)
            for i, z in enumerate(zs):
                set_row(z, d, lines[i * nx : (i + 1) * nx, :])
        for z in zs:
            set_row(z, row_s, field(s_ref, z))
            set_row(z, row_s + 1, field(f_ref, z))
            set_row(z, row_one, ones)
            set_row(z, row_d, nil)
            set_row(z, row_d + 1, nil)
            set_row(z, row_two, ones)

        def work(z):
            fds = tiles(z)
            h1, h2 = [], []
            yield from layers(z, fds, lg0_ref, h1, h2)
            for chunk in range(len(fds)):
                lanes = slice(chunk * xw * ny, (chunk + 1) * xw * ny)
                h1_ref[z, :, lanes] = h1[chunk]
                h2_ref[z, :, lanes] = h2[chunk]

        interleave([work(z) for z in zs], 3)
        return 0

    lax.fori_loop(0, nz // zb, start_body, 0)

    for copy in first:
        copy.wait()
    place_halo(4, xr_ref, yr_ref)

    def logit_cots(z, dcoup, ref):
        h_sf, h_sig = gates(get_log(ref, z, 0) + b_out_0)
        a_sf, a_sig = gates(get_log(ref, z, 1) + b_out_1)
        set_row(z, row_d, dcoup * a_sf * h_sig)
        set_row(z, row_d + 1, dcoup * h_sf * a_sig)
        return h_sf * a_sf

    def later_body(step, _):
        zs = [step * zb + i for i in range(zb)]
        lefts, rights = [], []

        def work(z):
            h_sf = gates(get_log(lg0_ref, z, 0) + b_out_0)[0]
            a_sf = gates(get_log(lg0_ref, z, 1) + b_out_1)[0]
            solid, fluid, free = field(s_ref, z), field(f_ref, z), field(free_ref, z)
            swap = free * (h_sf * a_sf) * (fluid - solid)
            solid_1 = solid + field(us_ref, z) * lap(solid, field(halo_ref, z)) + swap
            fluid_1 = fluid + field(us_ref, z, 1) * lap(fluid, field(halo_ref, z, 1)) - swap
            set_row(z, row_s, solid_1)
            set_row(z, row_s + 1, fluid_1)
            yield
            h1, h2 = [], []
            yield from layers(z, tiles(z), lg_ref, h1, h2)
            turn = free * (field(gs_ref, z) - field(gf_ref, z))
            swing = logit_cots(z, (fluid_1 - solid_1) * turn, lg_ref) * turn
            yield
            yield from layers_back(z, tiles(z), h1, h2, lefts, rights)
            new_s = field(gs_ref, z) + lap(field(ps_ref, z), field(halo_ref, z, 2)) - swing + get_log(lg_ref, z, 0)
            new_f = field(gf_ref, z) + lap(field(ps_ref, z, 1), field(halo_ref, z, 3)) + swing + get_log(lg_ref, z, 1)
            put_field(g2_ref, z, new_s)
            put_field(g2_ref, z, new_f, 1)
            put_field(ps_ref, z, field(us_ref, z) * new_s)
            put_field(ps_ref, z, field(us_ref, z, 1) * new_f, 1)

        interleave([work(z) for z in zs], 5)
        add_terms(lefts, rights)
        return 0

    lax.fori_loop(0, nz // zb, later_body, 0)

    stage_edges([(ps_ref, 0), (ps_ref, rows)], xs2_ref, ys2_ref)
    second = halo_copies(xs2_ref, xr2_ref, ys2_ref, yr2_ref, hs2_sem, hr2_sem)
    for copy in second:
        copy.start()

    def first_body(step, _):
        zs = [step * zb + i for i in range(zb)]
        lefts, rights = [], []

        def work(z):
            solid, fluid = field(s_ref, z), field(f_ref, z)
            set_row(z, row_s, solid)
            set_row(z, row_s + 1, fluid)
            turn = field(free_ref, z) * (field(g2_ref, z) - field(g2_ref, z, 1))
            swing = logit_cots(z, (fluid - solid) * turn, lg0_ref) * turn
            yield
            parts = [slice(i * xw * ny, (i + 1) * xw * ny) for i in range(nx // xw)]
            h1 = [h1_ref[z, :, lanes] for lanes in parts]
            h2 = [h2_ref[z, :, lanes] for lanes in parts]
            yield from layers_back(z, tiles(z), h1, h2, lefts, rights)
            put_field(g2_ref, z, field(g2_ref, z) - swing + get_log(lg_ref, z, 0))
            put_field(g2_ref, z, field(g2_ref, z, 1) + swing + get_log(lg_ref, z, 1), 1)

        interleave([work(z) for z in zs], 3)
        add_terms(lefts, rights)
        return 0

    lax.fori_loop(0, nz // zb, first_body, 0)

    piece = acc_ref.shape[1]
    lane = lax.broadcasted_iota(jnp.int32, (hid // 2, 2 * hid), 1)
    half = hid // 2
    wide_l = 2 * hid
    packed = jnp.concatenate(
        [
            grad_ref[0:TILE, 0:wide_l],
            jnp.where(
                lane >= hid,
                grad_ref[TILE : TILE + half, 0:wide_l],
                pltpu.roll(grad_ref[TILE + half : TILE + hid, 0:wide_l], hid, 1),
            ),
            grad_ref[TILE - LOG : TILE, wide_l : 2 * wide_l],
            jnp.zeros((ncol * piece - TILE - half - LOG, wide_l), f32),
        ],
        axis=0,
    )
    for i in range(ncol):
        acc_ref[i] = packed[i * piece : (i + 1) * piece, :]
    sends = []
    for k in range(1, ncol):
        dev = col_peer(k)
        sends.append(remote(acc_ref.at[dev[1]], part_ref.at[k - 1], c_ssem.at[k - 1], c_rsem.at[k - 1], dev))
    for copy in sends:
        copy.start()

    for copy in second:
        copy.wait()
    place_halo(2, xr2_ref, yr2_ref)

    for copy in sends:
        copy.wait()
    own = acc_ref[me_c]
    for k in range(ncol - 1):
        own = own + part_ref[k]
    grp_ref[me_g] = own
    sends = []
    for k in range(1, ngrp):
        sends.append(
            remote(grp_ref.at[me_g], grp_ref.at[me_g], g_ssem.at[k - 1], g_rsem.at[k - 1], grp_peer(k))
        )
    for copy in sends:
        copy.start()

    def final_body(z, _):
        adj_s_ref[pl.ds(pl.multiple_of(z * nx, nx), nx), :] = field(g2_ref, z) + lap(
            field(ps_ref, z), field(halo_ref, z)
        )
        adj_f_ref[pl.ds(pl.multiple_of(z * nx, nx), nx), :] = field(g2_ref, z, 1) + lap(
            field(ps_ref, z, 1), field(halo_ref, z, 1)
        )
        return 0

    lax.fori_loop(0, nz, final_body, 0, unroll=zb)
    stores = [
        pltpu.make_async_copy(adj_s_ref, out_s_ref, out_sem.at[0]),
        pltpu.make_async_copy(adj_f_ref, out_f_ref, out_sem.at[1]),
    ]
    for store in stores:
        store.start()

    for copy in sends:
        copy.wait()
    own = grp_ref[0]
    for k in range(1, ngrp):
        own = own + grp_ref[k]
    fin_ref[me_c] = own * scale
    sends = []
    for k in range(1, ncol):
        sends.append(remote(fin_ref.at[me_c], fin_ref.at[me_c], a_ssem.at[k - 1], a_rsem.at[k - 1], col_peer(k)))
    for copy in sends:
        copy.start()
    for copy in sends:
        copy.wait()
    for i in range(ncol):
        whole_ref[i * piece : (i + 1) * piece, :] = fin_ref[i]
    for store in stores:
        store.wait()


def unpack(
    ndesc, adj_s_ref, adj_f_ref, summed_ref, *refs
):
    targets, places, whole_ref, sem = refs[:8], refs[8:14], refs[14], refs[15]
    fetch = pltpu.make_async_copy(summed_ref, whole_ref, sem.at[8])
    fetch.start()
    copies = [
        pltpu.make_async_copy(source, target, sem.at[i])
        for i, (source, target) in enumerate(zip((adj_s_ref, adj_f_ref) + places, targets))
    ]
    copies[0].start()
    copies[1].start()
    g_w_in_ref, g_b_in_ref, g_w_mid_ref, g_b_mid_ref, g_w_out_ref, g_b_out_ref = places
    hid = g_w_mid_ref.shape[0]
    half, wide_l = hid // 2, 2 * hid
    row_one, row_d = ndesc + 2, ndesc + 3
    fetch.wait()
    whole = whole_ref[...]
    g_w_in_ref[...] = whole[0 : ndesc + 2, 0:hid]
    ones_row = whole[row_one : row_one + 1, :]
    g_b_in_ref[...] = ones_row[:, 0:hid]
    g_b_mid_ref[...] = pltpu.roll(ones_row, hid, 1)[:, 0:hid]
    mid = whole[TILE : TILE + half, :]
    g_w_mid_ref[0:half, :] = pltpu.roll(mid, hid, 1)[:, 0:hid]
    g_w_mid_ref[half:hid, :] = mid[:, 0:hid]
    at = TILE + half + row_d - (TILE - LOG)
    g_w_out_ref[...] = whole[at : at + 2, 0:hid]
    one_lane = hid + row_one
    b0 = pltpu.roll(whole[at : at + 1, :], wide_l - one_lane, 1)
    b1 = pltpu.roll(whole[at + 1 : at + 2, :], wide_l - one_lane + 1, 1)
    first_lane = lax.broadcasted_iota(jnp.int32, (1, wide_l), 1) == 0
    g_b_out_ref[...] = jnp.where(first_lane, b0, b1)[:, 0:2]
    for copy in copies[2:]:
        copy.start()
    for copy in copies:
        copy.wait()


def solution(mesh):
    ngrp, ncol = mesh.shape["grp"], mesh.shape["col"]

    def shards(
        descriptors, solid_temp, fluid_temp, material, fixed_mask, solid_cond, fluid_cond,
        w_in, b_in, w_mid, b_mid, w_out, b_out, solid_cot, fluid_cot,
    ):
        ndesc, nz, nx, ny = descriptors.shape
        feat, hid = w_in.shape
        rows = nz * nx
        zb = next(k for k in (4, 2, 1) if nz % k == 0)
        scale = loss_gain / math.sqrt(rows * ny * ngrp * ncol)
        used = TILE + hid // 2 + LOG
        piece = 8 * -(-used // (8 * ncol))
        flat = lambda a: a.reshape(rows, ny)
        vmem = pl.BlockSpec(memory_space=pltpu.VMEM)
        hbm = pl.BlockSpec(memory_space=pltpu.HBM)
        sds = jax.ShapeDtypeStruct
        fetched = (
            flat(fixed_mask), flat(material), solid_cond.reshape(1, -1), fluid_cond.reshape(1, -1),
            flat(solid_cot), flat(fluid_cot), flat(solid_temp), flat(fluid_temp),
            b_in.reshape(1, hid), b_mid.reshape(1, hid), w_mid, b_out.reshape(1, 2),
            descriptors.reshape(ndesc, rows, ny),
        )
        held = pl.pallas_call(
            functools.partial(kernel, ngrp, ncol, scale, zb),
            out_shape=(sds((rows, ny), f32), sds((rows, ny), f32), sds((ncol * piece, 2 * hid), f32)),
            in_specs=[vmem] * 2 + [hbm] * FETCHED,
            out_specs=(hbm, hbm, vmem),
            scratch_shapes=[pltpu.VMEM((rows, ny), f32), pltpu.VMEM((rows, ny), f32), pltpu.SemaphoreType.DMA((2,))]
            + [pltpu.VMEM(a.shape, a.dtype) for a in fetched]
            + [
                pltpu.SemaphoreType.DMA((FETCHED,)),
                pltpu.VMEM((128, 128), f32),
                pltpu.VMEM((rows * TILE, ny), f32),
                pltpu.VMEM((nz, hid, nx * ny), bf16),
                pltpu.VMEM((nz, hid, nx * ny), bf16),
                pltpu.VMEM((rows * LOG, ny), f32),
                pltpu.VMEM((rows * LOG, ny), f32),
                pltpu.VMEM((rows, ny), f32),
                pltpu.VMEM((2 * rows, ny), f32),
                pltpu.VMEM((2 * rows, ny), f32),
                pltpu.VMEM((2 * rows, ny), f32),
                pltpu.VMEM((4 * rows, ny), f32),
                pltpu.VMEM((TILE + hid, 4 * hid), f32),
                pltpu.VMEM((2, 4, nz, ny), f32),
                pltpu.VMEM((2, 4, nz, ny), f32),
                pltpu.VMEM((2, 4, rows), f32),
                pltpu.VMEM((2, 4, rows), f32),
                pltpu.VMEM((2, 2, nz, ny), f32),
                pltpu.VMEM((2, 2, nz, ny), f32),
                pltpu.VMEM((2, 2, rows), f32),
                pltpu.VMEM((2, 2, rows), f32),
                pltpu.VMEM((ncol, piece, 2 * hid), f32),
                pltpu.VMEM((ncol - 1, piece, 2 * hid), f32),
                pltpu.VMEM((ngrp, piece, 2 * hid), f32),
                pltpu.VMEM((ncol, piece, 2 * hid), f32),
                pltpu.SemaphoreType.DMA((4,)),
                pltpu.SemaphoreType.DMA((4,)),
                pltpu.SemaphoreType.DMA((4,)),
                pltpu.SemaphoreType.DMA((4,)),
                pltpu.SemaphoreType.DMA((ncol - 1,)),
                pltpu.SemaphoreType.DMA((ncol - 1,)),
                pltpu.SemaphoreType.DMA((ngrp - 1,)),
                pltpu.SemaphoreType.DMA((ngrp - 1,)),
                pltpu.SemaphoreType.DMA((ncol - 1,)),
                pltpu.SemaphoreType.DMA((ncol - 1,)),
            ],
            compiler_params=pltpu.CompilerParams(
                collective_id=0, has_side_effects=True, vmem_limit_bytes=64 * 1024 * 1024
            ),
            name="wick_adjoint",
        )(w_in, w_out.T, *fetched)
        shapes = (
            sds((rows, ny), f32), sds((rows, ny), f32), sds((feat, hid), f32), sds((1, hid), f32),
            sds((hid, hid), f32), sds((1, hid), f32), sds((2, hid), f32), sds((1, 2), f32),
        )
        outs = pl.pallas_call(
            functools.partial(unpack, ndesc),
            out_shape=shapes,
            in_specs=[hbm] * 3,
            out_specs=(hbm,) * 8,
            scratch_shapes=[pltpu.VMEM(a.shape, a.dtype) for a in shapes[2:]]
            + [pltpu.VMEM((ncol * piece, 2 * hid), f32), pltpu.SemaphoreType.DMA((9,))],
            compiler_params=pltpu.CompilerParams(vmem_limit_bytes=64 * 1024 * 1024),
            name="unpack",
        )(*held)
        block = lambda a: a.reshape(nz, nx, ny)
        return (
            block(outs[0]), block(outs[1]), outs[2], outs[3].reshape(hid),
            outs[4], outs[5].reshape(hid), outs[6].T, outs[7].reshape(2),
        )

    plane = P(None, "grp", "col")
    return jax.shard_map(
        shards,
        mesh=mesh,
        in_specs=(P(None, None, "grp", "col"),) + (plane,) * 4 + (P(),) * 8 + (plane,) * 2,
        out_specs=(plane, plane) + (P(),) * 6,
        check_vma=False,
    )
```

```python
import functools
import math

import jax
import jax.numpy as jnp
from jax import lax
from jax.experimental import pallas as pl
from jax.experimental.pallas import tpu as pltpu
from jax.sharding import PartitionSpec as P

time_step = 0.15
loss_gain = 16.0
MESH = pl.DeviceIdType.MESH
f32 = jnp.float32
bf16 = jnp.bfloat16
TILE = 16
LOG = 8
FETCHED = 13


def gates(logit):
    small = jnp.exp(-jnp.abs(logit))
    soft = jnp.maximum(logit, 0.0) + jnp.log1p(small)
    sig = jnp.where(logit >= 0.0, 1.0, small) / (1.0 + small)
    return soft, sig


def kernel(
    ngrp, ncol, scale, zb,
    w_in_ref, w_out_t_ref, *refs,
):
    sources, rest = refs[:FETCHED], refs[FETCHED:]
    (
    out_s_ref, out_f_ref, whole_ref, adj_s_ref, adj_f_ref, out_sem,
    mask_ref, mat_ref, scond_ref, fcond_ref, gs_ref, gf_ref, s_ref, f_ref,
    b_in_ref, b_mid_ref, w_mid_ref, b_out_ref, desc_ref, in_sem,
    aug_ref, fd_ref, h1_ref, h2_ref, lg0_ref, lg_ref, free_ref, us_ref, ps_ref, g2_ref,
    halo_ref, grad_ref, xs_ref, xr_ref, ys_ref, yr_ref, xs2_ref, xr2_ref, ys2_ref, yr2_ref,
    acc_ref, part_ref, grp_ref, fin_ref,
    hs_sem, hr_sem, hs2_sem, hr2_sem, c_ssem, c_rsem, g_ssem, g_rsem, a_ssem, a_rsem,
    ) = rest
    held = (
        mask_ref, mat_ref, scond_ref, fcond_ref, gs_ref, gf_ref, s_ref, f_ref,
        b_in_ref, b_mid_ref, w_mid_ref, b_out_ref, desc_ref,
    )
    fetches = [
        pltpu.make_async_copy(source, place, in_sem.at[i])
        for i, (source, place) in enumerate(zip(sources, held))
    ]
    for fetch in fetches:
        fetch.start()
    ndesc, _, ny = desc_ref.shape
    nz = xs_ref.shape[2]
    nx = s_ref.shape[0] // nz
    hid = w_mid_ref.shape[0]
    rows = nz * nx
    cells = nx * ny
    row_s, row_one, row_d, row_two = ndesc, ndesc + 2, ndesc + 3, ndesc + 5
    me_g = lax.axis_index("grp")
    me_c = lax.axis_index("col")

    def grp_peer(k):
        return (lax.rem(me_g + (k + ngrp), ngrp), me_c)

    def col_peer(k):
        return (me_g, lax.rem(me_c + (k + ncol), ncol))

    barrier = pltpu.get_barrier_semaphore()
    for k in range(1, ngrp):
        pl.semaphore_signal(barrier, inc=1, device_id=grp_peer(k), device_id_type=MESH)
    for k in range(1, ncol):
        pl.semaphore_signal(barrier, inc=1, device_id=col_peer(k), device_id_type=MESH)

    def remote(src, dst, ssem, rsem, peer):
        return pltpu.make_async_remote_copy(
            src_ref=src, dst_ref=dst, send_sem=ssem, recv_sem=rsem, device_id=peer, device_id_type=MESH
        )

    xi = lax.broadcasted_iota(jnp.int32, (nx, ny), 0)
    yi = lax.broadcasted_iota(jnp.int32, (nx, ny), 1)

    for fetch in fetches[:8]:
        fetch.wait()
    mat = mat_ref[...]
    free = time_step * (1.0 - mask_ref[...].astype(f32))
    free_ref[...] = free
    sk = jnp.zeros((rows, ny), f32)
    fk = jnp.zeros((rows, ny), f32)
    for kind in range(scond_ref.shape[1]):
        sk = sk + jnp.where(mat == kind, scond_ref[0:1, kind : kind + 1], 0.0)
        fk = fk + jnp.where(mat == kind, fcond_ref[0:1, kind : kind + 1], 0.0)
    us_ref[0:rows, :] = sk * free
    us_ref[rows : 2 * rows, :] = fk * free
    ps_ref[0:rows, :] = us_ref[0:rows, :] * gs_ref[...]
    ps_ref[rows : 2 * rows, :] = us_ref[rows : 2 * rows, :] * gf_ref[...]

    def stage_edges(refs, xsend, ysend):
        for i, (ref, base) in enumerate(refs):
            xsend[0, i] = ref[pl.ds(base, nz, stride=nx), :]
            xsend[1, i] = ref[pl.ds(base + nx - 1, nz, stride=nx), :]
            turned = jnp.transpose(ref[base : base + rows, :])
            ysend[0, i : i + 1, :] = turned[0:1, :]
            ysend[1, i : i + 1, :] = turned[ny - 1 : ny, :]

    def halo_copies(xsend, xrecv, ysend, yrecv, ssem, rsem):
        return [
            remote(xsend.at[0], xrecv.at[0], ssem.at[0], rsem.at[0], grp_peer(-1)),
            remote(xsend.at[1], xrecv.at[1], ssem.at[1], rsem.at[1], grp_peer(1)),
            remote(ysend.at[0], yrecv.at[0], ssem.at[2], rsem.at[2], col_peer(-1)),
            remote(ysend.at[1], yrecv.at[1], ssem.at[3], rsem.at[3], col_peer(1)),
        ]

    not_first_g = jnp.where(me_g == 0, 0.0, 1.0).astype(f32)
    not_last_g = jnp.where(me_g == ngrp - 1, 0.0, 1.0).astype(f32)
    not_first_c = jnp.where(me_c == 0, 0.0, 1.0).astype(f32)
    not_last_c = jnp.where(me_c == ncol - 1, 0.0, 1.0).astype(f32)

    def place_halo(count, xrecv, yrecv):
        line = lax.broadcasted_iota(jnp.int32, (ny, rows), 0)
        for i in range(count):
            low = yrecv[1, i : i + 1, :] * not_first_c
            high = yrecv[0, i : i + 1, :] * not_last_c
            edge = jnp.where(line == 0, low, 0.0) + jnp.where(line == ny - 1, high, 0.0)
            base = i * rows
            halo_ref[base : base + rows, :] = jnp.transpose(edge)
            at_low = pl.ds(base, nz, stride=nx)
            at_high = pl.ds(base + nx - 1, nz, stride=nx)
            halo_ref[at_low, :] = halo_ref[at_low, :] + xrecv[1, i] * not_first_g
            halo_ref[at_high, :] = halo_ref[at_high, :] + xrecv[0, i] * not_last_g

    def lap(v, halo):
        up = jnp.where(xi > 0, pltpu.roll(v, 1, 0), 0.0)
        down = jnp.where(xi < nx - 1, pltpu.roll(v, nx - 1, 0), 0.0)
        left = jnp.where(yi > 0, pltpu.roll(v, 1, 1), 0.0)
        right = jnp.where(yi < ny - 1, pltpu.roll(v, ny - 1, 1), 0.0)
        return (up + down) + (left + right) + halo - 4.0 * v

    stage_edges([(s_ref, 0), (f_ref, 0), (ps_ref, 0), (ps_ref, rows)], xs_ref, ys_ref)
    pl.semaphore_wait(barrier, ngrp + ncol - 2)
    first = halo_copies(xs_ref, xr_ref, ys_ref, yr_ref, hs_sem, hr_sem)
    for copy in first:
        copy.start()

    for fetch in fetches[8:]:
        fetch.wait()
    wide = aug_ref.shape[1]

    def split(b):
        high = b.astype(bf16).astype(f32)
        return high, b - high

    def turned_weights(pieces):
        aug_ref[...] = jnp.zeros(aug_ref.shape, f32)
        for at, value in pieces:
            aug_ref[at : at + value.shape[0], 0:hid] = value
        return jnp.transpose(aug_ref[...])

    b1_high, b1_low = split(b_in_ref[...])
    b2_high, b2_low = split(b_mid_ref[...])
    w_in = w_in_ref[...].astype(f32)
    w_out_t = w_out_t_ref[...].astype(f32)
    turned = turned_weights([(0, w_in), (row_one, b1_high), (row_two, b1_low), (TILE + row_d, w_out_t)])
    w1 = turned[0:hid, 0:TILE].astype(bf16)
    wo = turned[0:hid, TILE : 2 * TILE].astype(bf16)
    turned = turned_weights([(0, w_mid_ref[...].astype(f32)), (hid + row_one, b2_high), (hid + row_two, b2_low)])
    w2 = turned[0:hid, 0 : hid + TILE].astype(bf16)
    wm = w_mid_ref[...]
    aug_ref[...] = jnp.zeros(aug_ref.shape, f32)
    aug_ref[0:2, 0:hid] = w_out_t
    aug_ref[LOG : LOG + 2, 0:hid] = w_in[ndesc : ndesc + 2, :]
    w3 = aug_ref[0:LOG, 0:hid].astype(bf16)
    wd = aug_ref[LOG : 2 * LOG, 0:hid].astype(bf16)
    b_out_0 = jnp.broadcast_to(b_out_ref[0:1, 0:1], (nx, ny))
    b_out_1 = jnp.broadcast_to(b_out_ref[0:1, 1:2], (nx, ny))

    grad_ref[...] = jnp.zeros(grad_ref.shape, f32)

    def dot(a, b):
        return jnp.dot(a, b, preferred_element_type=f32)

    def set_row(z, row, value):
        fd_ref[pl.ds(pl.multiple_of(z * (nx * TILE), nx * TILE) + row, nx, stride=TILE), :] = value

    def tile(z):
        base = pl.multiple_of(z * (nx * TILE), nx * TILE)
        block = fd_ref[pl.ds(base, nx * TILE), :].astype(bf16)
        return jnp.concatenate([block[x * TILE : (x + 1) * TILE, :] for x in range(nx)], axis=1)

    def put_log(ref, z, value):
        for x in range(nx):
            at = pl.multiple_of(z * (nx * LOG), nx * LOG) + x * LOG
            ref[pl.ds(at, LOG), :] = value[:, x * ny : (x + 1) * ny]

    def get_log(ref, z, row):
        return ref[pl.ds(pl.multiple_of(z * (nx * LOG), nx * LOG) + row, nx, stride=LOG), :]

    def field(ref, z, which=0):
        return ref[pl.ds(pl.multiple_of(z * nx, nx) + which * rows, nx), :]

    def put_field(ref, z, value, which=0):
        ref[pl.ds(pl.multiple_of(z * nx, nx) + which * rows, nx), :] = value

    def layers(fds):
        h1 = [jnp.tanh(dot(w1, fd)).astype(bf16) for fd in fds]
        h2 = [jnp.tanh(dot(w2, jnp.concatenate([h, fd], axis=0))).astype(bf16) for h, fd in zip(h1, fds)]
        logits = [dot(w3, h) for h in h2]
        return h1, h2, logits

    def through(d, h):
        wide_h = h.astype(f32)
        return (d * (1.0 - wide_h * wide_h)).astype(bf16)

    def layers_back(fds, h1, h2, zs):
        d2 = [through(dot(wo, fd), h) for fd, h in zip(fds, h2)]
        d1 = [through(dot(wm, d), h) for d, h in zip(d2, h1)]
        for z, d in zip(zs, d1):
            put_log(lg_ref, z, dot(wd, d))
        total = grad_ref[:, 0 : 3 * hid + TILE]
        for i in range(len(zs)):
            left = jnp.concatenate([fds[i], h1[i]], axis=0)
            right = jnp.concatenate([d1[i], d2[i], h2[i], fds[i]], axis=0)
            total = total + lax.dot_general(
                left, right, (((1,), (1,)), ((), ())), preferred_element_type=f32
            )
        grad_ref[:, 0 : 3 * hid + TILE] = total

    ones = jnp.ones((nx, ny), f32)
    nil = jnp.zeros((nx, ny), f32)

    def start_body(step, _):
        zs = [step * zb + i for i in range(zb)]
        for d in range(ndesc):
            span = pl.ds(pl.multiple_of(step * (zb * nx), zb * nx), zb * nx)
            lines = desc_ref[d, span, :].astype(f32)
            for i, z in enumerate(zs):
                set_row(z, d, lines[i * nx : (i + 1) * nx, :])
        for z in zs:
            set_row(z, row_s, field(s_ref, z))
            set_row(z, row_s + 1, field(f_ref, z))
            set_row(z, row_one, ones)
            set_row(z, row_d, nil)
            set_row(z, row_d + 1, nil)
            set_row(z, row_two, ones)
        fds = [tile(z) for z in zs]
        h1, h2, logits = layers(fds)
        for z, a, b, c in zip(zs, h1, h2, logits):
            h1_ref[z] = a
            h2_ref[z] = b
            put_log(lg0_ref, z, c)
        return 0

    lax.fori_loop(0, nz // zb, start_body, 0)

    for copy in first:
        copy.wait()
    place_halo(4, xr_ref, yr_ref)

    def logit_cots(z, dcoup, ref):
        h_sf, h_sig = gates(get_log(ref, z, 0) + b_out_0)
        a_sf, a_sig = gates(get_log(ref, z, 1) + b_out_1)
        set_row(z, row_d, dcoup * a_sf * h_sig)
        set_row(z, row_d + 1, dcoup * h_sf * a_sig)
        return h_sf * a_sf

    def later_body(step, _):
        zs = [step * zb + i for i in range(zb)]
        diff = []
        for z in zs:
            h_sf = gates(get_log(lg0_ref, z, 0) + b_out_0)[0]
            a_sf = gates(get_log(lg0_ref, z, 1) + b_out_1)[0]
            solid, fluid, free = field(s_ref, z), field(f_ref, z), field(free_ref, z)
            swap = free * (h_sf * a_sf) * (fluid - solid)
            solid_1 = solid + field(us_ref, z) * lap(solid, field(halo_ref, z)) + swap
            fluid_1 = fluid + field(us_ref, z, 1) * lap(fluid, field(halo_ref, z, 1)) - swap
            set_row(z, row_s, solid_1)
            set_row(z, row_s + 1, fluid_1)
            diff.append(fluid_1 - solid_1)
        fds = [tile(z) for z in zs]
        h1, h2, logits = layers(fds)
        for z, c in zip(zs, logits):
            put_log(lg_ref, z, c)
        swing = []
        for z, d in zip(zs, diff):
            turn = field(free_ref, z) * (field(gs_ref, z) - field(gf_ref, z))
            swing.append(logit_cots(z, d * turn, lg_ref) * turn)
        fds = [tile(z) for z in zs]
        layers_back(fds, h1, h2, zs)
        for z, w in zip(zs, swing):
            new_s = field(gs_ref, z) + lap(field(ps_ref, z), field(halo_ref, z, 2)) - w + get_log(lg_ref, z, 0)
            new_f = field(gf_ref, z) + lap(field(ps_ref, z, 1), field(halo_ref, z, 3)) + w + get_log(lg_ref, z, 1)
            put_field(g2_ref, z, new_s)
            put_field(g2_ref, z, new_f, 1)
            put_field(ps_ref, z, field(us_ref, z) * new_s)
            put_field(ps_ref, z, field(us_ref, z, 1) * new_f, 1)
        return 0

    lax.fori_loop(0, nz // zb, later_body, 0)

    stage_edges([(ps_ref, 0), (ps_ref, rows)], xs2_ref, ys2_ref)
    second = halo_copies(xs2_ref, xr2_ref, ys2_ref, yr2_ref, hs2_sem, hr2_sem)
    for copy in second:
        copy.start()

    def first_body(step, _):
        zs = [step * zb + i for i in range(zb)]
        swing = []
        for z in zs:
            solid, fluid = field(s_ref, z), field(f_ref, z)
            set_row(z, row_s, solid)
            set_row(z, row_s + 1, fluid)
            turn = field(free_ref, z) * (field(g2_ref, z) - field(g2_ref, z, 1))
            swing.append(logit_cots(z, (fluid - solid) * turn, lg0_ref) * turn)
        fds = [tile(z) for z in zs]
        layers_back(fds, [h1_ref[z] for z in zs], [h2_ref[z] for z in zs], zs)
        for z, w in zip(zs, swing):
            put_field(g2_ref, z, field(g2_ref, z) - w + get_log(lg_ref, z, 0))
            put_field(g2_ref, z, field(g2_ref, z, 1) + w + get_log(lg_ref, z, 1), 1)
        return 0

    lax.fori_loop(0, nz // zb, first_body, 0)

    piece = acc_ref.shape[1]
    lane = lax.broadcasted_iota(jnp.int32, (hid // 2, 2 * hid), 1)
    half = hid // 2
    wide_l = 2 * hid
    packed = jnp.concatenate(
        [
            grad_ref[0:TILE, 0:wide_l],
            jnp.where(
                lane >= hid,
                grad_ref[TILE : TILE + half, 0:wide_l],
                pltpu.roll(grad_ref[TILE + half : TILE + hid, 0:wide_l], hid, 1),
            ),
            grad_ref[TILE - LOG : TILE, wide_l : 2 * wide_l],
            jnp.zeros((ncol * piece - TILE - half - LOG, wide_l), f32),
        ],
        axis=0,
    )
    for i in range(ncol):
        acc_ref[i] = packed[i * piece : (i + 1) * piece, :]
    sends = []
    for k in range(1, ncol):
        dev = col_peer(k)
        sends.append(remote(acc_ref.at[dev[1]], part_ref.at[k - 1], c_ssem.at[k - 1], c_rsem.at[k - 1], dev))
    for copy in sends:
        copy.start()

    for copy in second:
        copy.wait()
    place_halo(2, xr2_ref, yr2_ref)

    for copy in sends:
        copy.wait()
    own = acc_ref[me_c]
    for k in range(ncol - 1):
        own = own + part_ref[k]
    grp_ref[me_g] = own
    sends = []
    for k in range(1, ngrp):
        sends.append(
            remote(grp_ref.at[me_g], grp_ref.at[me_g], g_ssem.at[k - 1], g_rsem.at[k - 1], grp_peer(k))
        )
    for copy in sends:
        copy.start()

    def final_body(z, _):
        adj_s_ref[pl.ds(pl.multiple_of(z * nx, nx), nx), :] = field(g2_ref, z) + lap(
            field(ps_ref, z), field(halo_ref, z)
        )
        adj_f_ref[pl.ds(pl.multiple_of(z * nx, nx), nx), :] = field(g2_ref, z, 1) + lap(
            field(ps_ref, z, 1), field(halo_ref, z, 1)
        )
        return 0

    lax.fori_loop(0, nz, final_body, 0, unroll=zb)
    stores = [
        pltpu.make_async_copy(adj_s_ref, out_s_ref, out_sem.at[0]),
        pltpu.make_async_copy(adj_f_ref, out_f_ref, out_sem.at[1]),
    ]
    for store in stores:
        store.start()

    for copy in sends:
        copy.wait()
    own = grp_ref[0]
    for k in range(1, ngrp):
        own = own + grp_ref[k]
    fin_ref[me_c] = own * scale
    sends = []
    for k in range(1, ncol):
        sends.append(remote(fin_ref.at[me_c], fin_ref.at[me_c], a_ssem.at[k - 1], a_rsem.at[k - 1], col_peer(k)))
    for copy in sends:
        copy.start()
    for copy in sends:
        copy.wait()
    for i in range(ncol):
        whole_ref[i * piece : (i + 1) * piece, :] = fin_ref[i]
    for store in stores:
        store.wait()


def unpack(
    ndesc, adj_s_ref, adj_f_ref, summed_ref, *refs
):
    targets, places, held, in_sem, sem = refs[:8], refs[8:16], refs[16], refs[17], refs[18]
    sources = (summed_ref, adj_s_ref, adj_f_ref)
    fetches = [
        pltpu.make_async_copy(source, place, in_sem.at[i])
        for i, (source, place) in enumerate(zip(sources, (held, places[0], places[1])))
    ]
    for fetch in fetches:
        fetch.start()
    copies = [
        pltpu.make_async_copy(place, target, sem.at[i])
        for i, (place, target) in enumerate(zip(places, targets))
    ]
    fetches[0].wait()
    whole = held[...]
    g_w_in_ref, g_b_in_ref, g_w_mid_ref, g_b_mid_ref, g_w_out_ref, g_b_out_ref = places[2:]
    hid = g_w_mid_ref.shape[0]
    half, wide_l = hid // 2, 2 * hid
    row_one, row_d = ndesc + 2, ndesc + 3
    g_w_in_ref[...] = whole[0 : ndesc + 2, 0:hid]
    ones_row = whole[row_one : row_one + 1, :]
    g_b_in_ref[...] = ones_row[:, 0:hid]
    g_b_mid_ref[...] = pltpu.roll(ones_row, hid, 1)[:, 0:hid]
    mid = whole[TILE : TILE + half, :]
    g_w_mid_ref[0:half, :] = pltpu.roll(mid, hid, 1)[:, 0:hid]
    g_w_mid_ref[half:hid, :] = mid[:, 0:hid]
    at = TILE + half + row_d - (TILE - LOG)
    g_w_out_ref[...] = whole[at : at + 2, 0:hid]
    one_lane = hid + row_one
    b0 = pltpu.roll(whole[at : at + 1, :], wide_l - one_lane, 1)
    b1 = pltpu.roll(whole[at + 1 : at + 2, :], wide_l - one_lane + 1, 1)
    first_lane = lax.broadcasted_iota(jnp.int32, (1, wide_l), 1) == 0
    g_b_out_ref[...] = jnp.where(first_lane, b0, b1)[:, 0:2]
    for copy in copies[2:]:
        copy.start()
    for i in range(2):
        fetches[i + 1].wait()
        copies[i].start()
    for copy in copies:
        copy.wait()


def solution(mesh):
    ngrp, ncol = mesh.shape["grp"], mesh.shape["col"]

    def shards(
        descriptors, solid_temp, fluid_temp, material, fixed_mask, solid_cond, fluid_cond,
        w_in, b_in, w_mid, b_mid, w_out, b_out, solid_cot, fluid_cot,
    ):
        ndesc, nz, nx, ny = descriptors.shape
        feat, hid = w_in.shape
        rows = nz * nx
        zb = next(k for k in (4, 2, 1) if nz % k == 0)
        scale = loss_gain / math.sqrt(rows * ny * ngrp * ncol)
        used = TILE + hid // 2 + LOG
        piece = 8 * -(-used // (8 * ncol))
        flat = lambda a: a.reshape(rows, ny)
        vmem = pl.BlockSpec(memory_space=pltpu.VMEM)
        hbm = pl.BlockSpec(memory_space=pltpu.HBM)
        sds = jax.ShapeDtypeStruct
        fetched = (
            flat(fixed_mask), flat(material), solid_cond.reshape(1, -1), fluid_cond.reshape(1, -1),
            flat(solid_cot), flat(fluid_cot), flat(solid_temp), flat(fluid_temp),
            b_in.reshape(1, hid), b_mid.reshape(1, hid), w_mid, b_out.reshape(1, 2),
            descriptors.reshape(ndesc, rows, ny),
        )
        held = pl.pallas_call(
            functools.partial(kernel, ngrp, ncol, scale, zb),
            out_shape=(sds((rows, ny), f32), sds((rows, ny), f32), sds((ncol * piece, 2 * hid), f32)),
            in_specs=[vmem] * 2 + [hbm] * FETCHED,
            out_specs=(hbm, hbm, vmem),
            scratch_shapes=[pltpu.VMEM((rows, ny), f32), pltpu.VMEM((rows, ny), f32), pltpu.SemaphoreType.DMA((2,))]
            + [pltpu.VMEM(a.shape, a.dtype) for a in fetched]
            + [
                pltpu.SemaphoreType.DMA((FETCHED,)),
                pltpu.VMEM((128, 128), f32),
                pltpu.VMEM((rows * TILE, ny), f32),
                pltpu.VMEM((nz, hid, nx * ny), bf16),
                pltpu.VMEM((nz, hid, nx * ny), bf16),
                pltpu.VMEM((rows * LOG, ny), f32),
                pltpu.VMEM((rows * LOG, ny), f32),
                pltpu.VMEM((rows, ny), f32),
                pltpu.VMEM((2 * rows, ny), f32),
                pltpu.VMEM((2 * rows, ny), f32),
                pltpu.VMEM((2 * rows, ny), f32),
                pltpu.VMEM((4 * rows, ny), f32),
                pltpu.VMEM((TILE + hid, 4 * hid), f32),
                pltpu.VMEM((2, 4, nz, ny), f32),
                pltpu.VMEM((2, 4, nz, ny), f32),
                pltpu.VMEM((2, 4, rows), f32),
                pltpu.VMEM((2, 4, rows), f32),
                pltpu.VMEM((2, 2, nz, ny), f32),
                pltpu.VMEM((2, 2, nz, ny), f32),
                pltpu.VMEM((2, 2, rows), f32),
                pltpu.VMEM((2, 2, rows), f32),
                pltpu.VMEM((ncol, piece, 2 * hid), f32),
                pltpu.VMEM((ncol - 1, piece, 2 * hid), f32),
                pltpu.VMEM((ngrp, piece, 2 * hid), f32),
                pltpu.VMEM((ncol, piece, 2 * hid), f32),
                pltpu.SemaphoreType.DMA((4,)),
                pltpu.SemaphoreType.DMA((4,)),
                pltpu.SemaphoreType.DMA((4,)),
                pltpu.SemaphoreType.DMA((4,)),
                pltpu.SemaphoreType.DMA((ncol - 1,)),
                pltpu.SemaphoreType.DMA((ncol - 1,)),
                pltpu.SemaphoreType.DMA((ngrp - 1,)),
                pltpu.SemaphoreType.DMA((ngrp - 1,)),
                pltpu.SemaphoreType.DMA((ncol - 1,)),
                pltpu.SemaphoreType.DMA((ncol - 1,)),
            ],
            compiler_params=pltpu.CompilerParams(
                collective_id=0, has_side_effects=True, vmem_limit_bytes=64 * 1024 * 1024
            ),
            name="wick_adjoint",
        )(w_in, w_out.T, *fetched)
        shapes = (
            sds((rows, ny), f32), sds((rows, ny), f32), sds((feat, hid), f32), sds((1, hid), f32),
            sds((hid, hid), f32), sds((1, hid), f32), sds((2, hid), f32), sds((1, 2), f32),
        )
        outs = pl.pallas_call(
            functools.partial(unpack, ndesc),
            out_shape=shapes,
            in_specs=[hbm] * 3,
            out_specs=(hbm,) * 8,
            scratch_shapes=[pltpu.VMEM(a.shape, a.dtype) for a in shapes]
            + [
                pltpu.VMEM((ncol * piece, 2 * hid), f32),
                pltpu.SemaphoreType.DMA((3,)),
                pltpu.SemaphoreType.DMA((8,)),
            ],
            compiler_params=pltpu.CompilerParams(vmem_limit_bytes=64 * 1024 * 1024),
            name="unpack",
        )(*held)
        block = lambda a: a.reshape(nz, nx, ny)
        return (
            block(outs[0]), block(outs[1]), outs[2], outs[3].reshape(hid),
            outs[4], outs[5].reshape(hid), outs[6].T, outs[7].reshape(2),
        )

    plane = P(None, "grp", "col")
    return jax.shard_map(
        shards,
        mesh=mesh,
        in_specs=(P(None, None, "grp", "col"),) + (plane,) * 4 + (P(),) * 8 + (plane,) * 2,
        out_specs=(plane, plane) + (P(),) * 6,
        check_vma=False,
    )
```

```python
import functools
import math

import jax
import jax.numpy as jnp
from jax import lax
from jax.experimental import pallas as pl
from jax.experimental.pallas import tpu as pltpu
from jax.sharding import PartitionSpec as P

time_step = 0.15
loss_gain = 16.0
MESH = pl.DeviceIdType.MESH
f32 = jnp.float32
bf16 = jnp.bfloat16
TILE = 16
LOG = 8
FETCHED = 13


def gates(logit):
    small = jnp.exp(-jnp.abs(logit))
    soft = jnp.maximum(logit, 0.0) + jnp.log1p(small)
    sig = jnp.where(logit >= 0.0, 1.0, small) / (1.0 + small)
    return soft, sig


def kernel(
    ngrp, ncol, scale, zb,
    w_in_ref, w_out_t_ref, *refs,
):
    sources, rest = refs[:FETCHED], refs[FETCHED:]
    (
    out_s_ref, out_f_ref, whole_ref, adj_s_ref, adj_f_ref, out_sem,
    mask_ref, mat_ref, scond_ref, fcond_ref, gs_ref, gf_ref, s_ref, f_ref,
    b_in_ref, b_mid_ref, w_mid_ref, b_out_ref, desc_ref, in_sem,
    aug_ref, fd_ref, h1_ref, h2_ref, lg0_ref, lg_ref, free_ref, us_ref, ps_ref, g2_ref,
    halo_ref, grad_ref, xs_ref, xr_ref, ys_ref, yr_ref, xs2_ref, xr2_ref, ys2_ref, yr2_ref,
    acc_ref, part_ref, grp_ref, fin_ref,
    hs_sem, hr_sem, hs2_sem, hr2_sem, c_ssem, c_rsem, g_ssem, g_rsem, a_ssem, a_rsem,
    ) = rest
    held = (
        mask_ref, mat_ref, scond_ref, fcond_ref, gs_ref, gf_ref, s_ref, f_ref,
        b_in_ref, b_mid_ref, w_mid_ref, b_out_ref, desc_ref,
    )
    fetches = [
        pltpu.make_async_copy(source, place, in_sem.at[i])
        for i, (source, place) in enumerate(zip(sources, held))
    ]
    for fetch in fetches:
        fetch.start()
    ndesc, _, ny = desc_ref.shape
    nz = xs_ref.shape[2]
    nx = s_ref.shape[0] // nz
    hid = w_mid_ref.shape[0]
    rows = nz * nx
    row_s, row_one, row_d, row_two = ndesc, ndesc + 2, ndesc + 3, ndesc + 5
    me_g = lax.axis_index("grp")
    me_c = lax.axis_index("col")

    def grp_peer(k):
        return (lax.rem(me_g + (k + ngrp), ngrp), me_c)

    def col_peer(k):
        return (me_g, lax.rem(me_c + (k + ncol), ncol))

    barrier = pltpu.get_barrier_semaphore()
    for k in range(1, ngrp):
        pl.semaphore_signal(barrier, inc=1, device_id=grp_peer(k), device_id_type=MESH)
    for k in range(1, ncol):
        pl.semaphore_signal(barrier, inc=1, device_id=col_peer(k), device_id_type=MESH)

    def remote(src, dst, ssem, rsem, peer):
        return pltpu.make_async_remote_copy(
            src_ref=src, dst_ref=dst, send_sem=ssem, recv_sem=rsem, device_id=peer, device_id_type=MESH
        )

    xi = lax.broadcasted_iota(jnp.int32, (nx, ny), 0)
    yi = lax.broadcasted_iota(jnp.int32, (nx, ny), 1)

    for fetch in fetches[:8]:
        fetch.wait()
    mat = mat_ref[...]
    free = time_step * (1.0 - mask_ref[...].astype(f32))
    free_ref[...] = free
    sk = jnp.zeros((rows, ny), f32)
    fk = jnp.zeros((rows, ny), f32)
    for kind in range(scond_ref.shape[1]):
        sk = sk + jnp.where(mat == kind, scond_ref[0:1, kind : kind + 1], 0.0)
        fk = fk + jnp.where(mat == kind, fcond_ref[0:1, kind : kind + 1], 0.0)
    us_ref[0:rows, :] = sk * free
    us_ref[rows : 2 * rows, :] = fk * free
    ps_ref[0:rows, :] = us_ref[0:rows, :] * gs_ref[...]
    ps_ref[rows : 2 * rows, :] = us_ref[rows : 2 * rows, :] * gf_ref[...]

    def stage_edges(refs, xsend, ysend):
        for i, (ref, base) in enumerate(refs):
            xsend[0, i] = ref[pl.ds(base, nz, stride=nx), :]
            xsend[1, i] = ref[pl.ds(base + nx - 1, nz, stride=nx), :]
            turned = jnp.transpose(ref[base : base + rows, :])
            ysend[0, i : i + 1, :] = turned[0:1, :]
            ysend[1, i : i + 1, :] = turned[ny - 1 : ny, :]

    def halo_copies(xsend, xrecv, ysend, yrecv, ssem, rsem):
        return [
            remote(xsend.at[0], xrecv.at[0], ssem.at[0], rsem.at[0], grp_peer(-1)),
            remote(xsend.at[1], xrecv.at[1], ssem.at[1], rsem.at[1], grp_peer(1)),
            remote(ysend.at[0], yrecv.at[0], ssem.at[2], rsem.at[2], col_peer(-1)),
            remote(ysend.at[1], yrecv.at[1], ssem.at[3], rsem.at[3], col_peer(1)),
        ]

    not_first_g = jnp.where(me_g == 0, 0.0, 1.0).astype(f32)
    not_last_g = jnp.where(me_g == ngrp - 1, 0.0, 1.0).astype(f32)
    not_first_c = jnp.where(me_c == 0, 0.0, 1.0).astype(f32)
    not_last_c = jnp.where(me_c == ncol - 1, 0.0, 1.0).astype(f32)

    def place_halo(count, xrecv, yrecv):
        line = lax.broadcasted_iota(jnp.int32, (ny, rows), 0)
        for i in range(count):
            low = yrecv[1, i : i + 1, :] * not_first_c
            high = yrecv[0, i : i + 1, :] * not_last_c
            edge = jnp.where(line == 0, low, 0.0) + jnp.where(line == ny - 1, high, 0.0)
            base = i * rows
            halo_ref[base : base + rows, :] = jnp.transpose(edge)
            at_low = pl.ds(base, nz, stride=nx)
            at_high = pl.ds(base + nx - 1, nz, stride=nx)
            halo_ref[at_low, :] = halo_ref[at_low, :] + xrecv[1, i] * not_first_g
            halo_ref[at_high, :] = halo_ref[at_high, :] + xrecv[0, i] * not_last_g

    def lap(v, halo):
        up = jnp.where(xi > 0, pltpu.roll(v, 1, 0), 0.0)
        down = jnp.where(xi < nx - 1, pltpu.roll(v, nx - 1, 0), 0.0)
        left = jnp.where(yi > 0, pltpu.roll(v, 1, 1), 0.0)
        right = jnp.where(yi < ny - 1, pltpu.roll(v, ny - 1, 1), 0.0)
        return (up + down) + (left + right) + halo - 4.0 * v

    stage_edges([(s_ref, 0), (f_ref, 0), (ps_ref, 0), (ps_ref, rows)], xs_ref, ys_ref)
    pl.semaphore_wait(barrier, ngrp + ncol - 2)
    first = halo_copies(xs_ref, xr_ref, ys_ref, yr_ref, hs_sem, hr_sem)
    for copy in first:
        copy.start()

    for fetch in fetches[8:]:
        fetch.wait()
    wide = aug_ref.shape[1]

    def split(b):
        high = b.astype(bf16).astype(f32)
        return high, b - high

    def turned_weights(pieces):
        aug_ref[...] = jnp.zeros(aug_ref.shape, f32)
        for at, value in pieces:
            aug_ref[at : at + value.shape[0], 0:hid] = value
        return jnp.transpose(aug_ref[...])

    b1_high, b1_low = split(b_in_ref[...])
    b2_high, b2_low = split(b_mid_ref[...])
    w_in = w_in_ref[...].astype(f32)
    w_out_t = w_out_t_ref[...].astype(f32)
    turned = turned_weights([(0, w_in), (row_one, b1_high), (row_two, b1_low), (TILE + row_d, w_out_t)])
    w1 = turned[0:hid, 0:TILE].astype(bf16)
    wo = turned[0:hid, TILE : 2 * TILE].astype(bf16)
    turned = turned_weights([(0, w_mid_ref[...].astype(f32)), (hid + row_one, b2_high), (hid + row_two, b2_low)])
    w2 = turned[0:hid, 0 : hid + TILE].astype(bf16)
    wm = w_mid_ref[...]
    aug_ref[...] = jnp.zeros(aug_ref.shape, f32)
    aug_ref[0:2, 0:hid] = w_out_t
    aug_ref[LOG : LOG + 2, 0:hid] = w_in[ndesc : ndesc + 2, :]
    w3 = aug_ref[0:LOG, 0:hid].astype(bf16)
    wd = aug_ref[LOG : 2 * LOG, 0:hid].astype(bf16)
    b_out_0 = jnp.broadcast_to(b_out_ref[0:1, 0:1], (nx, ny))
    b_out_1 = jnp.broadcast_to(b_out_ref[0:1, 1:2], (nx, ny))

    grad_ref[...] = jnp.zeros(grad_ref.shape, f32)

    def dot(a, b):
        return jnp.dot(a, b, preferred_element_type=f32)

    def set_row(z, row, value):
        fd_ref[pl.ds(pl.multiple_of(z * (nx * TILE), nx * TILE) + row, nx, stride=TILE), :] = value

    def tile(z):
        base = pl.multiple_of(z * (nx * TILE), nx * TILE)
        block = fd_ref[pl.ds(base, nx * TILE), :].astype(bf16)
        return jnp.concatenate([block[x * TILE : (x + 1) * TILE, :] for x in range(nx)], axis=1)

    def put_log(ref, z, value):
        for x in range(nx):
            at = pl.multiple_of(z * (nx * LOG), nx * LOG) + x * LOG
            ref[pl.ds(at, LOG), :] = value[:, x * ny : (x + 1) * ny]

    def get_log(ref, z, row):
        return ref[pl.ds(pl.multiple_of(z * (nx * LOG), nx * LOG) + row, nx, stride=LOG), :]

    def field(ref, z, which=0):
        return ref[pl.ds(pl.multiple_of(z * nx, nx) + which * rows, nx), :]

    def put_field(ref, z, value, which=0):
        ref[pl.ds(pl.multiple_of(z * nx, nx) + which * rows, nx), :] = value

    cells = nx * ny

    def beside(values):
        return jnp.concatenate(values, axis=1)

    def layer_of(value, i):
        return value[:, i * cells : (i + 1) * cells]

    def layers(fd):
        h1 = jnp.tanh(dot(w1, fd)).astype(bf16)
        h2 = jnp.tanh(dot(w2, jnp.concatenate([h1, fd], axis=0))).astype(bf16)
        return h1, h2, dot(w3, h2)

    def through(d, h):
        wide_h = h.astype(f32)
        return (d * (1.0 - wide_h * wide_h)).astype(bf16)

    def layers_back(fd, h1, h2, zs):
        d2 = through(dot(wo, fd), h2)
        d1 = through(dot(wm, d2), h1)
        d_temps = dot(wd, d1)
        for i, z in enumerate(zs):
            put_log(lg_ref, z, layer_of(d_temps, i))
        left = jnp.concatenate([fd, h1], axis=0)
        right = jnp.concatenate([d1, d2, h2, fd], axis=0)
        grad_ref[:, 0 : 3 * hid + TILE] = grad_ref[:, 0 : 3 * hid + TILE] + lax.dot_general(
            left, right, (((1,), (1,)), ((), ())), preferred_element_type=f32
        )

    ones = jnp.ones((nx, ny), f32)
    nil = jnp.zeros((nx, ny), f32)

    def start_body(step, _):
        zs = [step * zb + i for i in range(zb)]
        for d in range(ndesc):
            span = pl.ds(pl.multiple_of(step * (zb * nx), zb * nx), zb * nx)
            lines = desc_ref[d, span, :].astype(f32)
            for i, z in enumerate(zs):
                set_row(z, d, lines[i * nx : (i + 1) * nx, :])
        for z in zs:
            set_row(z, row_s, field(s_ref, z))
            set_row(z, row_s + 1, field(f_ref, z))
            set_row(z, row_one, ones)
            set_row(z, row_d, nil)
            set_row(z, row_d + 1, nil)
            set_row(z, row_two, ones)
        h1, h2, logits = layers(beside([tile(z) for z in zs]))
        h1_ref[step] = h1
        h2_ref[step] = h2
        for i, z in enumerate(zs):
            put_log(lg0_ref, z, layer_of(logits, i))
        return 0

    lax.fori_loop(0, nz // zb, start_body, 0)

    for copy in first:
        copy.wait()
    place_halo(4, xr_ref, yr_ref)

    def logit_cots(z, dcoup, ref):
        h_sf, h_sig = gates(get_log(ref, z, 0) + b_out_0)
        a_sf, a_sig = gates(get_log(ref, z, 1) + b_out_1)
        set_row(z, row_d, dcoup * a_sf * h_sig)
        set_row(z, row_d + 1, dcoup * h_sf * a_sig)
        return h_sf * a_sf

    def later_body(step, _):
        zs = [step * zb + i for i in range(zb)]
        diff = []
        for z in zs:
            h_sf = gates(get_log(lg0_ref, z, 0) + b_out_0)[0]
            a_sf = gates(get_log(lg0_ref, z, 1) + b_out_1)[0]
            solid, fluid, free = field(s_ref, z), field(f_ref, z), field(free_ref, z)
            swap = free * (h_sf * a_sf) * (fluid - solid)
            solid_1 = solid + field(us_ref, z) * lap(solid, field(halo_ref, z)) + swap
            fluid_1 = fluid + field(us_ref, z, 1) * lap(fluid, field(halo_ref, z, 1)) - swap
            set_row(z, row_s, solid_1)
            set_row(z, row_s + 1, fluid_1)
            diff.append(fluid_1 - solid_1)
        h1, h2, logits = layers(beside([tile(z) for z in zs]))
        for i, z in enumerate(zs):
            put_log(lg_ref, z, layer_of(logits, i))
        swing = []
        for z, d in zip(zs, diff):
            turn = field(free_ref, z) * (field(gs_ref, z) - field(gf_ref, z))
            swing.append(logit_cots(z, d * turn, lg_ref) * turn)
        layers_back(beside([tile(z) for z in zs]), h1, h2, zs)
        for z, w in zip(zs, swing):
            new_s = field(gs_ref, z) + lap(field(ps_ref, z), field(halo_ref, z, 2)) - w + get_log(lg_ref, z, 0)
            new_f = field(gf_ref, z) + lap(field(ps_ref, z, 1), field(halo_ref, z, 3)) + w + get_log(lg_ref, z, 1)
            put_field(g2_ref, z, new_s)
            put_field(g2_ref, z, new_f, 1)
            put_field(ps_ref, z, field(us_ref, z) * new_s)
            put_field(ps_ref, z, field(us_ref, z, 1) * new_f, 1)
        return 0

    lax.fori_loop(0, nz // zb, later_body, 0)

    stage_edges([(ps_ref, 0), (ps_ref, rows)], xs2_ref, ys2_ref)
    second = halo_copies(xs2_ref, xr2_ref, ys2_ref, yr2_ref, hs2_sem, hr2_sem)
    for copy in second:
        copy.start()

    def first_body(step, _):
        zs = [step * zb + i for i in range(zb)]
        swing = []
        for z in zs:
            solid, fluid = field(s_ref, z), field(f_ref, z)
            set_row(z, row_s, solid)
            set_row(z, row_s + 1, fluid)
            turn = field(free_ref, z) * (field(g2_ref, z) - field(g2_ref, z, 1))
            swing.append(logit_cots(z, (fluid - solid) * turn, lg0_ref) * turn)
        layers_back(beside([tile(z) for z in zs]), h1_ref[step], h2_ref[step], zs)
        for z, w in zip(zs, swing):
            put_field(g2_ref, z, field(g2_ref, z) - w + get_log(lg_ref, z, 0))
            put_field(g2_ref, z, field(g2_ref, z, 1) + w + get_log(lg_ref, z, 1), 1)
        return 0

    lax.fori_loop(0, nz // zb, first_body, 0)

    piece = acc_ref.shape[1]
    lane = lax.broadcasted_iota(jnp.int32, (hid // 2, 2 * hid), 1)
    half = hid // 2
    wide_l = 2 * hid
    packed = jnp.concatenate(
        [
            grad_ref[0:TILE, 0:wide_l],
            jnp.where(
                lane >= hid,
                grad_ref[TILE : TILE + half, 0:wide_l],
                pltpu.roll(grad_ref[TILE + half : TILE + hid, 0:wide_l], hid, 1),
            ),
            grad_ref[TILE - LOG : TILE, wide_l : 2 * wide_l],
            jnp.zeros((ncol * piece - TILE - half - LOG, wide_l), f32),
        ],
        axis=0,
    )
    for i in range(ncol):
        acc_ref[i] = packed[i * piece : (i + 1) * piece, :]
    sends = []
    for k in range(1, ncol):
        dev = col_peer(k)
        sends.append(remote(acc_ref.at[dev[1]], part_ref.at[k - 1], c_ssem.at[k - 1], c_rsem.at[k - 1], dev))
    for copy in sends:
        copy.start()

    for copy in second:
        copy.wait()
    place_halo(2, xr2_ref, yr2_ref)

    for copy in sends:
        copy.wait()
    own = acc_ref[me_c]
    for k in range(ncol - 1):
        own = own + part_ref[k]
    grp_ref[me_g] = own
    sends = []
    for k in range(1, ngrp):
        sends.append(
            remote(grp_ref.at[me_g], grp_ref.at[me_g], g_ssem.at[k - 1], g_rsem.at[k - 1], grp_peer(k))
        )
    for copy in sends:
        copy.start()

    def final_body(z, _):
        adj_s_ref[pl.ds(pl.multiple_of(z * nx, nx), nx), :] = field(g2_ref, z) + lap(
            field(ps_ref, z), field(halo_ref, z)
        )
        adj_f_ref[pl.ds(pl.multiple_of(z * nx, nx), nx), :] = field(g2_ref, z, 1) + lap(
            field(ps_ref, z, 1), field(halo_ref, z, 1)
        )
        return 0

    lax.fori_loop(0, nz, final_body, 0, unroll=zb)
    stores = [
        pltpu.make_async_copy(adj_s_ref, out_s_ref, out_sem.at[0]),
        pltpu.make_async_copy(adj_f_ref, out_f_ref, out_sem.at[1]),
    ]
    for store in stores:
        store.start()

    for copy in sends:
        copy.wait()
    own = grp_ref[0]
    for k in range(1, ngrp):
        own = own + grp_ref[k]
    fin_ref[me_c] = own * scale
    sends = []
    for k in range(1, ncol):
        sends.append(remote(fin_ref.at[me_c], fin_ref.at[me_c], a_ssem.at[k - 1], a_rsem.at[k - 1], col_peer(k)))
    for copy in sends:
        copy.start()
    for copy in sends:
        copy.wait()
    for i in range(ncol):
        whole_ref[i * piece : (i + 1) * piece, :] = fin_ref[i]
    for store in stores:
        store.wait()


def unpack(
    ndesc, adj_s_ref, adj_f_ref, summed_ref, *refs
):
    targets, places, held, in_sem, sem = refs[:8], refs[8:16], refs[16], refs[17], refs[18]
    sources = (summed_ref, adj_s_ref, adj_f_ref)
    fetches = [
        pltpu.make_async_copy(source, place, in_sem.at[i])
        for i, (source, place) in enumerate(zip(sources, (held, places[0], places[1])))
    ]
    for fetch in fetches:
        fetch.start()
    copies = [
        pltpu.make_async_copy(place, target, sem.at[i])
        for i, (place, target) in enumerate(zip(places, targets))
    ]
    fetches[0].wait()
    whole = held[...]
    g_w_in_ref, g_b_in_ref, g_w_mid_ref, g_b_mid_ref, g_w_out_ref, g_b_out_ref = places[2:]
    hid = g_w_mid_ref.shape[0]
    half, wide_l = hid // 2, 2 * hid
    row_one, row_d = ndesc + 2, ndesc + 3
    g_w_in_ref[...] = whole[0 : ndesc + 2, 0:hid]
    ones_row = whole[row_one : row_one + 1, :]
    g_b_in_ref[...] = ones_row[:, 0:hid]
    g_b_mid_ref[...] = pltpu.roll(ones_row, hid, 1)[:, 0:hid]
    mid = whole[TILE : TILE + half, :]
    g_w_mid_ref[0:half, :] = pltpu.roll(mid, hid, 1)[:, 0:hid]
    g_w_mid_ref[half:hid, :] = mid[:, 0:hid]
    at = TILE + half + row_d - (TILE - LOG)
    g_w_out_ref[...] = whole[at : at + 2, 0:hid]
    one_lane = hid + row_one
    b0 = pltpu.roll(whole[at : at + 1, :], wide_l - one_lane, 1)
    b1 = pltpu.roll(whole[at + 1 : at + 2, :], wide_l - one_lane + 1, 1)
    first_lane = lax.broadcasted_iota(jnp.int32, (1, wide_l), 1) == 0
    g_b_out_ref[...] = jnp.where(first_lane, b0, b1)[:, 0:2]
    for copy in copies[2:]:
        copy.start()
    for i in range(2):
        fetches[i + 1].wait()
        copies[i].start()
    for copy in copies:
        copy.wait()


def solution(mesh):
    ngrp, ncol = mesh.shape["grp"], mesh.shape["col"]

    def shards(
        descriptors, solid_temp, fluid_temp, material, fixed_mask, solid_cond, fluid_cond,
        w_in, b_in, w_mid, b_mid, w_out, b_out, solid_cot, fluid_cot,
    ):
        ndesc, nz, nx, ny = descriptors.shape
        feat, hid = w_in.shape
        rows = nz * nx
        zb = next(k for k in (4, 2, 1) if nz % k == 0)
        scale = loss_gain / math.sqrt(rows * ny * ngrp * ncol)
        used = TILE + hid // 2 + LOG
        piece = 8 * -(-used // (8 * ncol))
        flat = lambda a: a.reshape(rows, ny)
        vmem = pl.BlockSpec(memory_space=pltpu.VMEM)
        hbm = pl.BlockSpec(memory_space=pltpu.HBM)
        sds = jax.ShapeDtypeStruct
        fetched = (
            flat(fixed_mask), flat(material), solid_cond.reshape(1, -1), fluid_cond.reshape(1, -1),
            flat(solid_cot), flat(fluid_cot), flat(solid_temp), flat(fluid_temp),
            b_in.reshape(1, hid), b_mid.reshape(1, hid), w_mid, b_out.reshape(1, 2),
            descriptors.reshape(ndesc, rows, ny),
        )
        held = pl.pallas_call(
            functools.partial(kernel, ngrp, ncol, scale, zb),
            out_shape=(sds((rows, ny), f32), sds((rows, ny), f32), sds((ncol * piece, 2 * hid), f32)),
            in_specs=[vmem] * 2 + [hbm] * FETCHED,
            out_specs=(hbm, hbm, vmem),
            scratch_shapes=[pltpu.VMEM((rows, ny), f32), pltpu.VMEM((rows, ny), f32), pltpu.SemaphoreType.DMA((2,))]
            + [pltpu.VMEM(a.shape, a.dtype) for a in fetched]
            + [
                pltpu.SemaphoreType.DMA((FETCHED,)),
                pltpu.VMEM((128, 128), f32),
                pltpu.VMEM((rows * TILE, ny), f32),
                pltpu.VMEM((nz // zb, hid, zb * nx * ny), bf16),
                pltpu.VMEM((nz // zb, hid, zb * nx * ny), bf16),
                pltpu.VMEM((rows * LOG, ny), f32),
                pltpu.VMEM((rows * LOG, ny), f32),
                pltpu.VMEM((rows, ny), f32),
                pltpu.VMEM((2 * rows, ny), f32),
                pltpu.VMEM((2 * rows, ny), f32),
                pltpu.VMEM((2 * rows, ny), f32),
                pltpu.VMEM((4 * rows, ny), f32),
                pltpu.VMEM((TILE + hid, 4 * hid), f32),
                pltpu.VMEM((2, 4, nz, ny), f32),
                pltpu.VMEM((2, 4, nz, ny), f32),
                pltpu.VMEM((2, 4, rows), f32),
                pltpu.VMEM((2, 4, rows), f32),
                pltpu.VMEM((2, 2, nz, ny), f32),
                pltpu.VMEM((2, 2, nz, ny), f32),
                pltpu.VMEM((2, 2, rows), f32),
                pltpu.VMEM((2, 2, rows), f32),
                pltpu.VMEM((ncol, piece, 2 * hid), f32),
                pltpu.VMEM((ncol - 1, piece, 2 * hid), f32),
                pltpu.VMEM((ngrp, piece, 2 * hid), f32),
                pltpu.VMEM((ncol, piece, 2 * hid), f32),
                pltpu.SemaphoreType.DMA((4,)),
                pltpu.SemaphoreType.DMA((4,)),
                pltpu.SemaphoreType.DMA((4,)),
                pltpu.SemaphoreType.DMA((4,)),
                pltpu.SemaphoreType.DMA((ncol - 1,)),
                pltpu.SemaphoreType.DMA((ncol - 1,)),
                pltpu.SemaphoreType.DMA((ngrp - 1,)),
                pltpu.SemaphoreType.DMA((ngrp - 1,)),
                pltpu.SemaphoreType.DMA((ncol - 1,)),
                pltpu.SemaphoreType.DMA((ncol - 1,)),
            ],
            compiler_params=pltpu.CompilerParams(
                collective_id=0, has_side_effects=True, vmem_limit_bytes=64 * 1024 * 1024
            ),
            name="wick_adjoint",
        )(w_in, w_out.T, *fetched)
        shapes = (
            sds((rows, ny), f32), sds((rows, ny), f32), sds((feat, hid), f32), sds((1, hid), f32),
            sds((hid, hid), f32), sds((1, hid), f32), sds((2, hid), f32), sds((1, 2), f32),
        )
        outs = pl.pallas_call(
            functools.partial(unpack, ndesc),
            out_shape=shapes,
            in_specs=[hbm] * 3,
            out_specs=(hbm,) * 8,
            scratch_shapes=[pltpu.VMEM(a.shape, a.dtype) for a in shapes]
            + [
                pltpu.VMEM((ncol * piece, 2 * hid), f32),
                pltpu.SemaphoreType.DMA((3,)),
                pltpu.SemaphoreType.DMA((8,)),
            ],
            compiler_params=pltpu.CompilerParams(vmem_limit_bytes=64 * 1024 * 1024),
            name="unpack",
        )(*held)
        block = lambda a: a.reshape(nz, nx, ny)
        return (
            block(outs[0]), block(outs[1]), outs[2], outs[3].reshape(hid),
            outs[4], outs[5].reshape(hid), outs[6].T, outs[7].reshape(2),
        )

    plane = P(None, "grp", "col")
    return jax.shard_map(
        shards,
        mesh=mesh,
        in_specs=(P(None, None, "grp", "col"),) + (plane,) * 4 + (P(),) * 8 + (plane,) * 2,
        out_specs=(plane, plane) + (P(),) * 6,
        check_vma=False,
    )
```
